256 devices in a mesh: seq: 32 (over z, x), tensor: 8 (over y, core).
Axes of the slice: x: 4, y: 4, z: 8, core: 2. Of those that a mesh axis runs over, the one named last changes fastest.
Arguments:
- resid: bfloat16 [4096, 4096], P('seq', 'tensor'), may hold values from -40 to 40
- queries: bfloat16 [4096, 4096], P('seq', 'tensor'), may hold values from -8 to 8
- keys: bfloat16 [4096, 4096], P('seq', 'tensor'), may hold values from -6 to 6
- values: bfloat16 [4096, 4096], P('seq', 'tensor'), may hold values from -18 to 18
- doc_ids: int32 [4096], P('seq'), may hold values from 0 to 3, never falling along the last dimension, each value on 1 to 2048 neighbouring positions
- modality: int32 [4096], P('seq'), may hold values from 0 to 2, as said below
- norm_gain: float32 [3, 4096], P(None, 'tensor'), may hold values from 0.1 to 1.9
- gate_w: bfloat16 [4096, 3, 11008], P('tensor', None, 'seq'), may hold values from -0.09375 to 0.09375
- up_w: bfloat16 [4096, 3, 11008], P('tensor', None, 'seq'), may hold values from -0.09375 to 0.09375
- down_weight_matrix: bfloat16 [3, 11008, 4096], P(None, 'seq', 'tensor'), may hold values from -0.0546875 to 0.0546875
Outputs:
- layer_out: bfloat16 [4096, 4096], P('seq', 'tensor')
The draws below stay inside these ranges and needn't reach their ends.
Inputs may be any that keep to these rules, and one draw needn't show every extreme that they name: `modality`: in each shard of 128 consecutive tokens, at most 48 tokens carry any one tag; in every draw some shard has exactly 48 tokens with tag 0.
All inputs are finite; a program needn't handle non-finite values.
Results may differ from the reference program's by a relative error of at most 0.018.
Values may be sent and summed in bfloat16 or wider, within the bound.
A program may use at most 64 MiB of HBM per device.

```python
import math
import jax
import jax.numpy as jnp
import numpy as np
from jax import lax

D = 4096
HEADS = 32
FF = 11008
DH = 128
MODS = 3
DOCS = 4
TOK_DEV = 128
TOKENS = 4096
CAP = 48
N_TENSOR = 8


def query_key_pair(key):
    base = jax.random.fold_in(key, 9)
    key_query, key_keys = jax.random.split(base, 2)
    query_draw = jnp.clip(jax.random.normal(key_query, (TOKENS, D), jnp.float32), -6.0, 6.0)
    key_draw = jnp.clip(jax.random.normal(key_keys, (TOKENS, D), jnp.float32), -6.0, 6.0)
    return (query_draw, key_draw)


def draw_queries(key, part):
    return query_key_pair(key)[0].astype(jnp.bfloat16)


def draw_keys(key, part):
    return query_key_pair(key)[1].astype(jnp.bfloat16)


def draw_resid(key, part):
    base = jax.random.fold_in(key, 3)
    key_normal, key_column = jax.random.split(base, 2)
    entries = jnp.clip(jax.random.normal(key_normal, (TOKENS, D), jnp.float32), -5.0, 5.0)
    ramp = jnp.arange(D, dtype=jnp.float32) / D
    jitter = jax.random.uniform(key_column, (D,), minval=0.5, maxval=1.5)
    columns = 0.3 * 3.0 ** ramp * jitter
    return (entries * columns[None, :]).astype(jnp.bfloat16)


def draw_modality(key, part):
    base = jax.random.fold_in(key, 11)
    key_text, key_image, key_full, key_perm = jax.random.split(base, 4)
    shards = TOKENS // TOK_DEV
    text_low = max(0, TOK_DEV - 2 * CAP)
    text_count = jax.random.randint(key_text, (shards,), text_low, CAP + 1)
    full_shard = jax.random.randint(key_full, (), 0, shards)
    text_count = jnp.where(jnp.arange(shards, dtype=jnp.int32) == full_shard, CAP, text_count)
    remaining = TOK_DEV - text_count
    lowest = jnp.maximum(0, remaining - CAP)
    highest = jnp.minimum(CAP, remaining)
    image_count = lowest + jax.random.randint(key_image, (shards,), 0, 1 << 20) % (highest - lowest + 1)
    slot_index = jnp.arange(TOK_DEV, dtype=jnp.int32)[None, :]
    ordered = jnp.where(slot_index < text_count[:, None], 0, jnp.where(slot_index < (text_count + image_count)[:, None], 1, 2)).astype(jnp.int32)
    perm_keys = jax.random.split(key_perm, shards)
    orders = jax.vmap(lambda one_key: jax.random.permutation(one_key, TOK_DEV))(perm_keys)
    shuffled = jnp.take_along_axis(ordered, orders, axis=1)
    return shuffled.reshape(TOKENS).astype(jnp.int32)


def block_scale(own_key, dims, cuts, least, largest):
    gain, own = 1.0, jax.random.fold_in(own_key, 6)
    for dim, shards_of in cuts:
        heights = jnp.exp(jax.random.uniform(jax.random.fold_in(own, dim), (shards_of,), jnp.float32, least / len(cuts), largest / len(cuts)))
        gain = gain * jnp.repeat(heights, dims[dim] // shards_of).reshape([-1 if axis == dim else 1 for axis in range(len(dims))])
    return gain


def length_profile(number_of, total, most, skew):
    weights = [(1 << 20) // math.isqrt(standing ** skew) + 1 for standing in range(2, number_of + 1)]
    rest, given = total - most - (number_of - 1), [1] * (number_of - 1)
    while rest > 0:
        movable = [i for i in range(number_of - 1) if given[i] < most]
        whole, left = sum([weights[i] for i in movable]), rest
        for i in movable:
            more = min(most - given[i], max(1, left * weights[i] // whole), rest)
            given[i] = given[i] + more
            rest = rest - more
    return np.array([most] + given)


def ragged_sizes(stream_key, number_of, total, most, slope):
    if number_of == 2:
        one = jax.random.randint(stream_key, (), max(1, total - most), min(most, total - 1) + 1)
        return jnp.stack([one, total - one])
    sizes = jnp.asarray(length_profile(number_of, total, most, slope), jnp.int32)
    twos = (number_of - 1) // 2
    source_of, sink = sizes[1:1 + 2 * twos:2], sizes[2:2 + 2 * twos:2]
    margin = jnp.minimum(source_of - 1, most - sink)
    moved = jax.random.randint(jax.random.fold_in(stream_key, 1), (twos,), 0, 1 << 20) % (margin + 1)
    sizes = sizes.at[1:1 + 2 * twos:2].set(source_of - moved).at[2:2 + 2 * twos:2].set(sink + moved)
    return sizes[jax.random.permutation(jax.random.fold_in(stream_key, 2), number_of)]


def normal_values(stream_key, extent, scale, reach, cuts=(), held_as=jnp.bfloat16):
    values = scale * jax.random.normal(stream_key, extent, jnp.float32)
    if cuts:
        values = values * block_scale(stream_key, extent, cuts, -0.22, 0.18)
    return jnp.clip(values, -reach, reach).astype(held_as)


def setup_inputs(seed: int = 0) -> dict:
    arg_keys = jax.random.split(jax.random.key(seed), 11)
    resid = draw_resid(jax.random.fold_in(arg_keys[10], 71), 0)
    queries = draw_queries(jax.random.fold_in(arg_keys[10], 71), 0)
    keys = draw_keys(jax.random.fold_in(arg_keys[10], 71), 0)
    values = normal_values(arg_keys[3], (TOKENS, D), 3.0, 18.0, ((0, 32), (1, 8)))
    doc_ids = jnp.searchsorted(jnp.cumsum(ragged_sizes(arg_keys[4], DOCS, TOKENS, TOKENS // 2, 0)), jnp.arange(TOKENS), side="right").astype(jnp.int32)
    modality = draw_modality(jax.random.fold_in(arg_keys[10], 71), 0)
    norm_gain = jnp.clip(1.0 + 0.18 * jax.random.normal(arg_keys[6], (MODS, D), jnp.float32), 0.1, 1.9)
    gate_w = normal_values(arg_keys[7], (D, MODS, FF), D ** -0.5, 0.09375, ((0, 8), (2, 32)))
    up_w = normal_values(arg_keys[8], (D, MODS, FF), D ** -0.5, 0.09375, ((0, 8), (2, 32)))
    down_weight_matrix = normal_values(arg_keys[9], (MODS, FF, D), FF ** -0.5, 0.0546875, ((1, 32), (2, 8)))
    return dict(resid=resid, queries=queries, keys=keys, values=values, doc_ids=doc_ids, modality=modality, norm_gain=norm_gain, gate_w=gate_w, up_w=up_w, down_weight_matrix=down_weight_matrix)


def reference(resid, queries, keys, values, doc_ids, modality, norm_gain, gate_w, up_w, down_weight_matrix):
    positions = jnp.arange(TOKENS, dtype=jnp.int32)
    allowed = (positions[None, :] <= positions[:, None]) & (doc_ids[None, :] == doc_ids[:, None])
    scale_factor = 1.0 / math.sqrt(DH)

    def head_attend(operands):
        q_head, k_head, v_head = operands
        scores = jnp.dot(q_head, k_head.T, preferred_element_type=jnp.float32) * scale_factor
        scores = jnp.where(allowed, scores, -1e+30)
        row_max = lax.optimization_barrier(jnp.max(scores, axis=1, keepdims=True))
        powers = jnp.where(allowed, jnp.exp(scores - row_max), 0.0)
        totals = lax.optimization_barrier(jnp.sum(powers, axis=1, keepdims=True))
        blended = jnp.dot(powers.astype(jnp.bfloat16), v_head, preferred_element_type=jnp.float32)
        return blended / totals

    def split_heads(matrix):
        return matrix.reshape(TOKENS, HEADS, DH).transpose(1, 0, 2)
    per_head = lax.map(head_attend, (split_heads(queries), split_heads(keys), split_heads(values)))
    attended = per_head.transpose(1, 0, 2).reshape(TOKENS, D).astype(jnp.bfloat16)
    stream = resid.astype(jnp.float32) + attended.astype(jnp.float32)
    inv_rms = lax.rsqrt(lax.optimization_barrier(jnp.mean(stream * stream, axis=1, keepdims=True)) + 1e-05)
    normalized_input = (stream * inv_rms * norm_gain[modality]).astype(jnp.bfloat16)
    shards = TOKENS // TOK_DEV
    tag_rows = modality.reshape(shards, TOK_DEV)
    onehot = (tag_rows[:, :, None] == jnp.arange(3, dtype=jnp.int32)[None, None, :]).astype(jnp.int32)
    slot_rank = lax.optimization_barrier(jnp.sum(onehot * (jnp.cumsum(onehot, axis=1) - 1), axis=2))
    normed_rows = normalized_input.reshape(shards, TOK_DEV, D).astype(jnp.float32)
    block_width = D // N_TENSOR
    ffn_sum = jnp.zeros((shards, TOK_DEV, D), jnp.float32)
    for served in range(MODS):
        placing = ((tag_rows == served)[:, None, :] & (slot_rank[:, None, :] == jnp.arange(CAP, dtype=jnp.int32)[None, :, None])).astype(jnp.float32)
        buffer = jnp.einsum('scr,srf->scf', placing, normed_rows, precision=lax.Precision.HIGHEST)
        buffer = buffer.astype(jnp.bfloat16).reshape(shards * CAP, D)
        gate_slab = gate_w[:, served, :]
        up_weight_block = up_w[:, served, :]
        down_slab = down_weight_matrix[served]

        def add_block(block_index, running):
            offset = (block_index * block_width).astype(jnp.int32)
            inputs = lax.dynamic_slice_in_dim(buffer, offset, block_width, 1)
            gate_rows = lax.dynamic_slice_in_dim(gate_slab, offset, block_width, 0)
            up_rows = lax.dynamic_slice_in_dim(up_weight_block, offset, block_width, 0)
            gate_piece = jnp.dot(inputs, gate_rows, preferred_element_type=jnp.float32).astype(jnp.bfloat16)
            up_piece = jnp.dot(inputs, up_rows, preferred_element_type=jnp.float32).astype(jnp.bfloat16)
            gate_piece, up_piece = lax.optimization_barrier((gate_piece, up_piece))
            return (running[0] + gate_piece.astype(jnp.float32), running[1] + up_piece.astype(jnp.float32))
        empty_total = jnp.zeros((shards * CAP, FF), jnp.float32)
        gate_sum, up_sum = lax.fori_loop(0, N_TENSOR, add_block, (empty_total, empty_total))
        hidden = (jax.nn.silu(gate_sum) * up_sum).astype(jnp.bfloat16)
        slot_part = jnp.dot(hidden, down_slab, preferred_element_type=jnp.float32).reshape(shards, CAP, D)
        ffn_sum = ffn_sum + jnp.einsum('scr,scf->srf', placing, slot_part, precision=lax.Precision.HIGHEST)
    return (stream + ffn_sum.reshape(TOKENS, D)).astype(jnp.bfloat16)
```

```python
import math

import jax
import jax.numpy as jnp
from jax import lax
from jax.experimental import pallas as pl
from jax.experimental.pallas import tpu as pltpu
from jax.sharding import Mesh
from jax.sharding import PartitionSpec as P

D = 4096
DH = 128
MODS = 3
CAP = 48
ROWS = 128
NZ, NX, NY = 8, 4, 4
BACK = 4
UNITS, WIDE = 344, 384
SEQ = ("z", "x")
TENSOR = ("y", "c")
MESH = pl.DeviceIdType.MESH
F32, BF16 = jnp.float32, jnp.bfloat16


def around(i, by, n):
    return lax.rem(i + (by % n), n)


class Wire:
    def __init__(self, send, recv):
        self.send, self.recv, self.copies = send, recv, []

    def __call__(self, src, dst, to):
        k = len(self.copies)
        copy = pltpu.make_async_remote_copy(
            src_ref=src,
            dst_ref=dst,
            send_sem=self.send.at[k],
            recv_sem=self.recv.at[k],
            device_id=to,
            device_id_type=MESH,
        )
        self.copies.append(copy)
        copy.start()
        return copy

    def drain(self):
        for copy in self.copies:
            copy.wait_send()


def greet(partners):
    barrier = pltpu.get_barrier_semaphore()
    for partner in partners:
        pl.semaphore_signal(barrier, inc=1, device_id=partner, device_id_type=MESH)
    pl.semaphore_wait(barrier, len(partners))


def eye():
    return lax.broadcasted_iota(jnp.int32, (ROWS, ROWS), 0) == lax.broadcasted_iota(
        jnp.int32, (ROWS, ROWS), 1
    )


def to_column(row):
    return jnp.sum(jnp.where(eye(), row, jnp.zeros_like(row)), axis=1, keepdims=True)


def to_row(column):
    return jnp.sum(jnp.where(eye(), column, jnp.zeros_like(column)), axis=0, keepdims=True)


def attend_kernel(
    q_ref, k_ref, v_ref, resid_ref, docs_ref, tags_ref, gain_ref,
    slots_ref, stream_ref,
    qb, kb, vb, db, dcol, top, total, acc, ab, att, sqb, send, recv,
):
    z, x = lax.axis_index("z"), lax.axis_index("x")
    y, c = lax.axis_index("y"), lax.axis_index("c")
    t = 2 * y + c
    tensor_peers = [around(t, o, 8) for o in range(1, 8)]
    tensor_peers = [{"y": p // 2, "c": lax.rem(p, 2)} for p in tensor_peers]
    x_peers = [around(x, o, NX) for o in (1, 3, 2)]
    up, down = {"z": around(z, 1, NZ)}, {"z": around(z, -1, NZ)}
    greet([{"x": p} for p in x_peers] + [up, down] + tensor_peers)
    wire = Wire(send, recv)

    coming = []
    for p in x_peers:
        cols = pl.ds(pl.multiple_of(p * DH, DH), DH)
        coming.append(wire(k_ref.at[:, cols], kb.at[0, x], {"x": p}))
        coming.append(wire(v_ref.at[:, cols], vb.at[0, x], {"x": p}))
        coming.append(wire(docs_ref, db.at[0, x], {"x": p}))
        coming.append(wire(q_ref.at[:, cols], qb.at[x], {"x": p}))
    own = pl.ds(pl.multiple_of(x * DH, DH), DH)
    kb[0, x] = k_ref[:, own]
    vb[0, x] = v_ref[:, own]
    qb[x] = q_ref[:, own]
    db[0, x] = docs_ref[...]
    for copy in coming:
        copy.wait_recv()

    for j in range(NX):
        dcol[j] = to_column(db[0, j])
    scale = 1.0 / math.sqrt(DH)
    for d in range(BACK + 1):
        if d > 0:
            for copy in moving:
                copy.wait_recv()
        if d < BACK:
            moving = [wire(b.at[d], b.at[d + 1], up) for b in (kb, vb, db)]
        first_key = around(z, -d, NZ) * (NX * ROWS)
        keys = kb[d].reshape(NX * ROWS, DH)
        vals = vb[d].reshape(NX * ROWS, DH)
        key_docs = jnp.concatenate([db[d, j] for j in range(NX)], axis=1)

        def block(j, _, d=d, first_key=first_key, keys=keys, vals=vals, key_docs=key_docs):
            score = (
                lax.dot_general(
                    qb[j], keys, (((1,), (1,)), ((), ())), preferred_element_type=F32
                )
                * scale
            )
            query_pos = (z * NX + j) * ROWS + lax.broadcasted_iota(jnp.int32, score.shape, 0)
            key_pos = first_key + lax.broadcasted_iota(jnp.int32, score.shape, 1)
            allowed = (key_pos <= query_pos) & (key_docs == dcol[j])
            score = jnp.where(allowed, score, -1e30)
            high = jnp.max(score, axis=1, keepdims=True)
            if d > 0:
                old = top[j]
                high = jnp.maximum(high, old)
            power = jnp.where(allowed, jnp.exp(score - high), 0.0)
            add = jnp.sum(power, axis=1, keepdims=True)
            blend = jnp.dot(power.astype(BF16), vals, preferred_element_type=F32)
            if d > 0:
                fade = jnp.exp(old - high)
                add = add + fade * total[j]
                blend = blend + fade * acc[j]
            top[j] = high
            total[j] = add
            acc[j] = blend
            if d == BACK:
                ab[j] = (blend / add).astype(BF16)
            return _

        lax.fori_loop(0, NX, block, 0)

    coming = [wire(ab.at[p], att.at[x], {"x": p}) for p in x_peers]
    att[x] = ab[x]
    tag_row = tags_ref[...]
    tag_col = to_column(tag_row)
    for copy in coming:
        copy.wait_recv()
    stream = resid_ref[...].astype(F32) + jnp.concatenate(
        [att[j].astype(F32) for j in range(NX)], axis=1
    )
    stream_ref[...] = stream
    sqb[t] = to_row(jnp.sum(stream * stream, axis=1, keepdims=True))
    coming = [wire(sqb.at[t], sqb.at[t], p) for p in tensor_peers]
    rank = jnp.sum(
        jnp.where(
            (tag_col == tag_row)
            & (
                lax.broadcasted_iota(jnp.int32, (ROWS, ROWS), 0)
                < lax.broadcasted_iota(jnp.int32, (ROWS, ROWS), 1)
            ),
            1.0,
            0.0,
        ),
        axis=0,
        keepdims=True,
    ).astype(jnp.int32)
    slot = lax.broadcasted_iota(jnp.int32, (CAP, ROWS), 0)
    gain = jnp.where(
        tag_col == 0, gain_ref[0:1, :], jnp.where(tag_col == 1, gain_ref[1:2, :], gain_ref[2:3, :])
    )
    scaled = stream
    for copy in coming:
        copy.wait_recv()
    squares = jnp.sum(sqb[...], axis=0)
    inv = to_column(lax.rsqrt(squares / D + 1e-5))
    normed = (scaled * inv * gain).astype(BF16)
    for m in range(MODS):
        placing = jnp.where((tag_row == m) & (rank == slot), 1.0, 0.0).astype(BF16)
        slots_ref[m] = jnp.dot(placing, normed, preferred_element_type=F32).astype(BF16)
    wire.drain()


def gather(wire, axis, n, me, view):
    half = n // 2
    for s in range(1, half + 1):
        last = s == half
        right, left = view(around(me, 1 - s, n), 0 if last else None), view(
            around(me, s - 1, n), 1 if last else None
        )
        moving = [
            wire(right, right, {axis: around(me, 1, n)}),
            wire(left, left, {axis: around(me, -1, n)}),
        ]
        yield
        for copy in moving:
            copy.wait_recv()


def summed(a, b):
    return (a.astype(F32) + b.astype(F32)).astype(BF16)


def scatter(wire, axis, n, me, view, landing, put):
    half = n // 2
    for s in range(1, half + 1):
        far = half - s + 1
        part = (0, 1) if s == 1 else (None, None)
        to = (around(me, far, n), around(me, -far, n))
        if s > 1:
            before = (0, 1) if s == 2 else (None, None)
            for side in (0, 1):
                total = view(to[side], before[side])
                total[...] = summed(total[...], landing(side, s - 1, before[side])[...])
        moving = [
            wire(view(to[side], part[side]), landing(side, s, part[side]), {axis: around(me, by, n)})
            for side, by in ((0, 1), (1, -1))
        ]
        yield
        for copy in moving:
            copy.wait_recv()
    put(
        view(me, None)[...].astype(F32)
        + landing(0, half, None)[...].astype(F32)
        + landing(1, half, None)[...].astype(F32)
    )


def together(*processes):
    active = list(processes)
    while active:
        active = [p for p in active if next(p, "end") != "end"]
        if active:
            yield


def cut(base, part):
    return pl.ds(base, 256) if part is None else pl.ds(base + 128 * part, 128)


def ffn_kernel(
    slots_ref, gate_ref, up_ref, down_ref, stream_ref, tags_ref,
    out_ref,
    xb, pb, cr, ya, yb, hb, yo, za, xa, zc, xc, fin, send, recv,
):
    z, x = lax.axis_index("z"), lax.axis_index("x")
    y, c = lax.axis_index("y"), lax.axis_index("c")
    other = {"c": 1 - c}
    y_right, y_left = {"y": around(y, 1, NY)}, {"y": around(y, -1, NY)}
    greet(
        [{"x": around(x, o, NX)} for o in (1, -1)]
        + [{"z": around(z, o, NZ)} for o in (1, -1)]
        + [y_right, y_left, other]
    )
    wire = Wire(send, recv)
    for m in range(MODS):
        xb[m, z, x] = slots_ref[m]

    def gather_first(m):
        yield from gather(wire, "x", NX, x, lambda j, p: xb.at[m, z, j, :, cut(0, p)])
        yield from gather(wire, "z", NZ, z, lambda j, p: xb.at[m, j, :, :, cut(0, p)])

    def gather_second(m):
        yield from gather(wire, "z", NZ, z, lambda j, p: xb.at[m, j, x, :, cut(256, p)])
        yield from gather(wire, "x", NX, x, lambda j, p: xb.at[m, :, j, :, cut(256, p)])

    def partial(m, plane):
        rows = xb[m, plane].reshape(NX * CAP, 512)
        for k, w_ref in enumerate((gate_ref, up_ref)):
            pb[m, plane, :, k * WIDE : k * WIDE + UNITS] = lax.dot_general(
                rows, w_ref[m], (((1,), (1,)), ((), ())), preferred_element_type=F32
            ).astype(BF16)

    def down_product(m, plane):
        part = jnp.dot(hb[m, plane][:, :UNITS], down_ref[m], preferred_element_type=F32)
        yo[m, plane] = part.astype(BF16).reshape(NX, CAP, 512)

    def middle(m):
        mine = {o: 2 * around(y, o, NY) + c for o in range(NY)}
        theirs = {o: 2 * around(y, o, NY) + 1 - c for o in range(NY)}
        order = (2, 1, 3, 0)
        core = {}
        for o in order:
            partial(m, theirs[o])
            core[o] = wire(pb.at[m, theirs[o]], cr.at[m, o], other)
        yield
        for o in order:
            partial(m, mine[o])
        yield
        for o in order[:3]:
            core[o].wait_recv()
            pb[m, mine[o]] = summed(pb[m, mine[o]], cr[m, o])
            if o == 2:
                moving = [
                    wire(pb.at[m, mine[2], :, pl.ds(0, WIDE)], ya.at[m, 0], y_right),
                    wire(pb.at[m, mine[2], :, pl.ds(WIDE, WIDE)], ya.at[m, 1], y_left),
                ]
        yield
        for copy in moving:
            copy.wait_recv()
        pb[m, mine[1], :, 0:WIDE] = summed(pb[m, mine[1], :, 0:WIDE], ya[m, 0])
        moving = [wire(pb.at[m, mine[1]], yb.at[m, 0], y_right)]
        pb[m, mine[3], :, WIDE:] = summed(pb[m, mine[3], :, WIDE:], ya[m, 1])
        moving.append(wire(pb.at[m, mine[3]], yb.at[m, 1], y_left))
        core[0].wait_recv()
        yield
        for copy in moving:
            copy.wait_recv()
        both = (
            pb[m, mine[0]].astype(F32)
            + cr[m, 0].astype(F32)
            + yb[m, 0].astype(F32)
            + yb[m, 1].astype(F32)
        )
        gate, up = both[:, :WIDE], both[:, WIDE:]
        hb[m, mine[0]] = (gate / (1.0 + jnp.exp(-gate)) * up).astype(BF16)

        def pass_on(plane, to, rows=None):
            ref = hb.at[m, plane] if rows is None else hb.at[m, plane, pl.ds(rows, 96)]
            return wire(ref, ref, to)

        moving = [pass_on(mine[0], y_right), pass_on(mine[0], y_left)]
        across = [pass_on(mine[0], other)]
        down_product(m, mine[0])
        yield
        for copy in moving:
            copy.wait_recv()
        moving = [pass_on(mine[3], y_right, 0), pass_on(mine[1], y_left, 96)]
        across += [pass_on(mine[3], other), pass_on(mine[1], other)]
        down_product(m, mine[3])
        down_product(m, mine[1])
        yield
        for copy in moving:
            copy.wait_recv()
        across.append(pass_on(mine[2], other))
        down_product(m, mine[2])
        for copy, o in zip(across, (0, 3, 1, 2)):
            copy.wait_recv()
            down_product(m, theirs[o])
        yield

    def scatter_first(m):
        def put_z(value):
            yo[m, z, :, :, 0:256] = value.astype(BF16)

        def put(value):
            fin[m, :, 0:256] = value.astype(BF16)

        yield from scatter(
            wire, "z", NZ, z,
            lambda j, p: yo.at[m, j, :, :, cut(0, p)],
            lambda side, s, p: za.at[m, side, s - 1, :, :, cut(0, p)],
            put_z,
        )
        yield from scatter(
            wire, "x", NX, x,
            lambda j, p: yo.at[m, z, j, :, cut(0, p)],
            lambda side, s, p: xa.at[m, side, s - 1, :, cut(0, p)],
            put,
        )

    def scatter_second(m):
        def put_x(value):
            yo[m, :, x, :, 256:512] = value.astype(BF16)

        def put(value):
            fin[m, :, 256:512] = value.astype(BF16)

        yield from scatter(
            wire, "x", NX, x,
            lambda j, p: yo.at[m, :, j, :, cut(256, p)],
            lambda side, s, p: xc.at[m, side, s - 1, :, :, cut(0, p)],
            put_x,
        )
        yield from scatter(
            wire, "z", NZ, z,
            lambda j, p: yo.at[m, j, x, :, cut(256, p)],
            lambda side, s, p: zc.at[m, side, s - 1, :, cut(0, p)],
            put,
        )

    for phase in range(MODS + 2):
        work = []
        if 0 <= phase - 2 < MODS:
            work += [scatter_first(phase - 2), scatter_second(phase - 2)]
        if 0 <= phase - 1 < MODS:
            work.append(middle(phase - 1))
        if phase < MODS:
            work += [gather_first(phase), gather_second(phase)]
        for _ in together(*work):
            pass

    tag_row = tags_ref[...]
    tag_col = to_column(tag_row)
    rank = jnp.sum(
        jnp.where(
            (tag_col == tag_row)
            & (
                lax.broadcasted_iota(jnp.int32, (ROWS, ROWS), 1)
                < lax.broadcasted_iota(jnp.int32, (ROWS, ROWS), 0)
            ),
            1.0,
            0.0,
        ),
        axis=1,
        keepdims=True,
    ).astype(jnp.int32)
    slot = lax.broadcasted_iota(jnp.int32, (ROWS, CAP), 1)
    result = stream_ref[...]
    for m in range(MODS):
        placing = jnp.where((tag_col == m) & (rank == slot), 1.0, 0.0).astype(BF16)
        result = result + jnp.dot(placing, fin[m], preferred_element_type=F32)
    out_ref[...] = result.astype(BF16)
    wire.drain()


def on_device(resid, queries, keys, values, doc_ids, modality, norm_gain, gate_w, up_w, down_w):
    vmem = pl.BlockSpec(memory_space=pltpu.VMEM)
    tags = modality.reshape(1, ROWS)
    block = (NX, ROWS, DH)
    slots, stream = pl.pallas_call(
        attend_kernel,
        out_shape=(
            jax.ShapeDtypeStruct((MODS, CAP, 512), BF16),
            jax.ShapeDtypeStruct((ROWS, 512), F32),
        ),
        in_specs=[vmem] * 7,
        out_specs=(vmem, vmem),
        scratch_shapes=[
            pltpu.VMEM(block, BF16),
            pltpu.VMEM((BACK + 1, *block), BF16),
            pltpu.VMEM((BACK + 1, *block), BF16),
            pltpu.VMEM((BACK + 1, NX, 1, ROWS), jnp.int32),
            pltpu.VMEM((NX, ROWS, 1), jnp.int32),
            pltpu.VMEM((NX, ROWS, 1), F32),
            pltpu.VMEM((NX, ROWS, 1), F32),
            pltpu.VMEM(block, F32),
            pltpu.VMEM(block, BF16),
            pltpu.VMEM(block, BF16),
            pltpu.VMEM((8, 1, ROWS), F32),
            pltpu.SemaphoreType.DMA((40,)),
            pltpu.SemaphoreType.DMA((40,)),
        ],
        compiler_params=pltpu.CompilerParams(
            collective_id=0, has_side_effects=True, vmem_limit_bytes=32 << 20
        ),
        name="attend",
    )(queries, keys, values, resid, doc_ids.reshape(1, ROWS), tags, norm_gain)
    return pl.pallas_call(
        ffn_kernel,
        out_shape=jax.ShapeDtypeStruct((ROWS, 512), BF16),
        in_specs=[vmem] * 6,
        out_specs=vmem,
        scratch_shapes=[
            pltpu.VMEM((MODS, NZ, NX, CAP, 512), BF16),
            pltpu.VMEM((MODS, 8, NX * CAP, 2 * WIDE), BF16),
            pltpu.VMEM((MODS, NY, NX * CAP, 2 * WIDE), BF16),
            pltpu.VMEM((MODS, 2, NX * CAP, WIDE), BF16),
            pltpu.VMEM((MODS, 2, NX * CAP, 2 * WIDE), BF16),
            pltpu.VMEM((MODS, 8, NX * CAP, WIDE), BF16),
            pltpu.VMEM((MODS, NZ, NX, CAP, 512), BF16),
            pltpu.VMEM((MODS, 2, NZ // 2, NX, CAP, 256), BF16),
            pltpu.VMEM((MODS, 2, NX // 2, CAP, 256), BF16),
            pltpu.VMEM((MODS, 2, NZ // 2, CAP, 256), BF16),
            pltpu.VMEM((MODS, 2, NX // 2, NZ, CAP, 256), BF16),
            pltpu.VMEM((MODS, CAP, 512), BF16),
            pltpu.SemaphoreType.DMA((220,)),
            pltpu.SemaphoreType.DMA((220,)),
        ],
        compiler_params=pltpu.CompilerParams(
            collective_id=1, has_side_effects=True, vmem_limit_bytes=60 << 20
        ),
        name="ffn",
    )(
        slots,
        gate_w.transpose(1, 2, 0),
        up_w.transpose(1, 2, 0),
        down_w,
        stream,
        tags,
    )


def solution(mesh):
    split = Mesh(mesh.devices.reshape(NZ, NX, NY, 2), ("z", "x", "y", "c"))
    placed = (
        P(SEQ, TENSOR),
        P(SEQ, TENSOR),
        P(SEQ, TENSOR),
        P(SEQ, TENSOR),
        P(SEQ),
        P(SEQ),
        P(None, TENSOR),
        P(TENSOR, None, SEQ),
        P(TENSOR, None, SEQ),
        P(None, SEQ, TENSOR),
    )
    return jax.shard_map(
        on_device, mesh=split, in_specs=placed, out_specs=P(SEQ, TENSOR), check_vma=False
    )
```

```python
import math

import jax
import jax.numpy as jnp
from jax import lax
from jax.experimental import pallas as pl
from jax.experimental.pallas import tpu as pltpu
from jax.sharding import Mesh
from jax.sharding import PartitionSpec as P

D = 4096
DH = 128
MODS = 3
CAP = 48
ROWS = 128
NZ, NX, NY = 8, 4, 4
BACK = 4
TURNED = 3
UNITS, WIDE = 344, 384
HALF = 256
STAGGER = 1
SEQ = ("z", "x")
TENSOR = ("y", "c")
MESH = pl.DeviceIdType.MESH
F32, BF16 = jnp.float32, jnp.bfloat16


def around(i, by, n):
    return lax.rem(i + (by % n), n)


class Wire:
    def __init__(self, send, recv):
        self.send, self.recv, self.copies = send, recv, []

    def __call__(self, src, dst, to):
        k = len(self.copies)
        copy = pltpu.make_async_remote_copy(
            src_ref=src,
            dst_ref=dst,
            send_sem=self.send.at[k],
            recv_sem=self.recv.at[k],
            device_id=to,
            device_id_type=MESH,
        )
        self.copies.append(copy)
        copy.start()
        return copy

    def drain(self):
        for copy in self.copies:
            copy.wait_send()


def landed(copies):
    for copy in copies:
        copy.wait_recv()


def greet(partners):
    barrier = pltpu.get_barrier_semaphore()
    for partner in partners:
        pl.semaphore_signal(barrier, inc=1, device_id=partner, device_id_type=MESH)
    pl.semaphore_wait(barrier, len(partners))


def iota(shape, dim):
    return lax.broadcasted_iota(jnp.int32, shape, dim)


def eye():
    return iota((ROWS, ROWS), 0) == iota((ROWS, ROWS), 1)


def to_column(row):
    return jnp.sum(jnp.where(eye(), row, jnp.zeros_like(row)), axis=1, keepdims=True)


def to_row(column):
    return jnp.sum(jnp.where(eye(), column, jnp.zeros_like(column)), axis=0, keepdims=True)


def attend(wire, here, refs, fetch, xb, stream, scratch):
    z, x, y, c = here
    q_ref, k_ref, v_ref, resid_ref, docs_ref, tags_ref, gain_ref = refs
    qb, kb, vb, kr, vr, db, dcol, top, total, acc, ab, att, sqb, resid, tags, gain = scratch
    t = 2 * y + c
    up, down = {"z": around(z, 1, NZ)}, {"z": around(z, -1, NZ)}
    order = (2, 1, 3, 0)
    at = {o: around(x, o, NX) for o in order}

    def cols(p):
        return pl.ds(pl.multiple_of(p * DH, DH), DH)

    local = [
        fetch(k_ref.at[:, cols(x)], kb.at[0, x]),
        fetch(v_ref.at[:, cols(x)], vb.at[0, x]),
        fetch(docs_ref, db.at[0, x]),
        fetch(q_ref.at[:, cols(x)], qb.at[x]),
        fetch(tags_ref, tags),
        fetch(gain_ref, gain),
        fetch(resid_ref, resid),
    ]
    coming = {"k": [], "v": [], "q": []}
    for o in order[:3]:
        coming["k"].append(wire(k_ref.at[:, cols(at[o])], kb.at[0, x], {"x": at[o]}))
    for o in order[:3]:
        coming["v"].append(wire(v_ref.at[:, cols(at[o])], vb.at[0, x], {"x": at[o]}))
    for o in order[:3]:
        coming["q"].append(wire(docs_ref, db.at[0, x], {"x": at[o]}))
        coming["q"].append(wire(q_ref.at[:, cols(at[o])], qb.at[x], {"x": at[o]}))

    near = pl.ds(0, TURNED)
    rest = pl.ds(TURNED, NX - TURNED)

    def forward(b, r, d):
        if d == BACK:
            return []
        if d + 1 < BACK:
            moving = [wire(b.at[d], b.at[d + 1], up)]
        else:
            moving = [wire(b.at[d, rest], b.at[d + 1, rest], up)]
        source = b.at[0, near] if d == 0 else r.at[d - 1]
        target = b.at[BACK, near] if d + 1 == BACK else r.at[d]
        return moving + [wire(source, target, down)]

    local[0].wait()
    landed(coming["k"])
    moving_k = forward(kb, kr, 0)
    local[1].wait()
    landed(coming["v"])
    moving_v = forward(vb, vr, 0)
    local[2].wait()
    local[3].wait()
    landed(coming["q"])
    moving_d = [wire(db.at[0], db.at[1], up)]
    for o in order:
        dcol[at[o]] = to_column(db[0, at[o]])
    factor = math.log2(math.e) / math.sqrt(DH)
    returned = []

    def block(d, o):
        j = at[o]
        keys = kb[d].reshape(NX * ROWS, DH)
        vals = vb[d].reshape(NX * ROWS, DH)
        key_docs = jnp.concatenate([db[d, i] for i in range(NX)], axis=1)
        score = lax.dot_general(
            qb[j], keys, (((1,), (1,)), ((), ())), preferred_element_type=F32
        )
        if d == 0:
            allowed = (iota(score.shape, 1) <= j * ROWS + iota(score.shape, 0)) & (
                key_docs == dcol[j]
            )
        else:
            allowed = jnp.where(z < d, -1, key_docs) == dcol[j]
        score = jnp.where(allowed, score, -1e30)
        high = jnp.max(score, axis=1, keepdims=True)
        if d > 0:
            old = top[j]
            high = jnp.maximum(high, old)
        power = jnp.exp2((score - high) * factor)
        add = jnp.sum(power, axis=1, keepdims=True)
        blend = jnp.dot(power.astype(BF16), vals, preferred_element_type=F32)
        if d > 0:
            fade = jnp.exp2((old - high) * factor)
            add = add + fade * total[j]
            blend = blend + fade * acc[j]
        if d < BACK:
            top[j] = high
            total[j] = add
            acc[j] = blend
            return
        result = (blend / add).astype(BF16)
        if o == 0:
            att[x] = result
        else:
            ab[j] = result
            returned.append(wire(ab.at[j], att.at[x], {"x": j}))

    for d in range(1, BACK + 1):
        landed(moving_k)
        moving_k = forward(kb, kr, d)
        block(d - 1, 2)
        block(d - 1, 1)
        landed(moving_v)
        moving_v = forward(vb, vr, d)
        landed(moving_d)
        if d < BACK:
            moving_d = [wire(db.at[d], db.at[d + 1], up)]
        block(d - 1, 3)
        block(d - 1, 0)
    for o in order:
        block(BACK, o)

    for copy in local[4:]:
        copy.wait()
    tag_row = tags[...]
    tag_col = to_column(tag_row)
    rank = jnp.sum(
        jnp.where(
            (tag_col == tag_row) & (iota((ROWS, ROWS), 0) < iota((ROWS, ROWS), 1)), 1.0, 0.0
        ),
        axis=0,
        keepdims=True,
    ).astype(jnp.int32)
    slot = iota((CAP, ROWS), 0)
    landed(returned)
    flow = resid[...].astype(F32) + jnp.concatenate(
        [att[i].astype(F32) for i in range(NX)], axis=1
    )
    stream[...] = flow
    sqb[t] = to_row(jnp.sum(flow * flow, axis=1, keepdims=True))
    peers = [around(t, o, 8) for o in range(1, 8)]
    coming = [wire(sqb.at[t], sqb.at[t], {"y": lax.div(p, 2), "c": lax.rem(p, 2)}) for p in peers]
    gains = jnp.where(
        tag_col == 0, gain[0:1, :], jnp.where(tag_col == 1, gain[1:2, :], gain[2:3, :])
    )
    landed(coming)
    inv = to_column(lax.rsqrt(jnp.sum(sqb[...], axis=0) / D + 1e-5))
    normed = (flow * inv * gains).astype(BF16)
    for m in range(MODS):
        placing = jnp.where((tag_row == m) & (rank == slot), 1.0, 0.0).astype(BF16)
        xb[m, lax.div(z, 2), lax.rem(z, 2), x] = jnp.dot(
            placing, normed, preferred_element_type=F32
        ).astype(BF16)


def gather(wire, axis, n, me, view):
    half = n // 2
    for s in range(1, half + 1):
        last = s == half
        right = view(around(me, 1 - s, n), 0 if last else None)
        left = view(around(me, s - 1, n), 1 if last else None)
        moving = [
            wire(right, right, {axis: around(me, 1, n)}),
            wire(left, left, {axis: around(me, -1, n)}),
        ]
        yield
        landed(moving)


def gather_at_once(wire, axis, n, me, view):
    far = sorted(range(1, n), key=lambda o: -min(o, n - o))
    moving = [wire(view(me, None), view(me, None), {axis: around(me, o, n)}) for o in far]
    yield
    landed(moving)


def scatter(wire, axis, n, me, view, landing, put):
    half = n // 2
    for s in range(1, half + 1):
        far = half - s + 1
        part = (0, 1) if s == 1 else (None, None)
        to = (around(me, far, n), around(me, -far, n))
        if s > 1:
            before = (0, 1) if s == 2 else (None, None)
            for side in (0, 1):
                total = view(to[side], before[side])
                total[...] = total[...] + landing(side * half + s - 2, before[side])[...]
        moving = [
            wire(
                view(to[side], part[side]),
                landing(side * half + s - 1, part[side]),
                {axis: around(me, by, n)},
            )
            for side, by in ((0, 1), (1, -1))
        ]
        yield
        landed(moving)
    put(
        view(me, None)[...].astype(F32)
        + landing(half - 1, None)[...].astype(F32)
        + landing(n - 1, None)[...].astype(F32)
    )


def scatter_at_once(wire, axis, n, me, view, landing, put):
    far = sorted(range(1, n), key=lambda o: -min(o, n - o))
    moving = [
        wire(view(around(me, o, n), None), landing(o, None), {axis: around(me, o, n)}) for o in far
    ]
    yield
    landed(moving)
    total = view(me, None)[...].astype(F32)
    for o in range(1, n):
        total = total + landing(o, None)[...].astype(F32)
    put(total)


def together(*processes):
    active = list(processes)
    while active:
        active = [p for p in active if next(p, "end") != "end"]
        if active:
            yield


def cut(base, part):
    return pl.ds(base, HALF) if part is None else pl.ds(base + 128 * part, 128)


def feed_forward(wire, here, weights, xb, scratch):
    z, x, y, c = here
    pb, cr, ya, yb, hb, yo, za, xa, zc, xc, fin = scratch
    gate_w, up_w, down_w, ready = weights
    other = {"c": 1 - c}
    y_right, y_left = {"y": around(y, 1, NY)}, {"y": around(y, -1, NY)}

    def plane(j):
        return lax.div(j, 2), lax.rem(j, 2)

    def gather_first(m):
        yield from gather_at_once(
            wire, "x", NX, x, lambda j, p: xb.at[(m, *plane(z), j, slice(None), cut(0, p))]
        )
        yield from gather(
            wire, "z", NZ, z,
            lambda j, p: xb.at[(m, *plane(j), slice(None), slice(None), cut(0, p))],
        )

    def gather_second(m):
        way = gather_at_once if m == 0 else gather
        yield from way(
            wire, "z", NZ, z, lambda j, p: xb.at[(m, *plane(j), x, slice(None), cut(HALF, p))]
        )
        yield from gather(wire, "x", NX, x, lambda j, p: xb.at[m, :, :, j, :, cut(HALF, p)])

    def partial(m, core, k):
        rows = xb[m, :, core].reshape(NY * NX * CAP, 512)
        value = lax.dot_general(
            rows, (gate_w, up_w)[k][m], (((1,), (1,)), ((), ())), preferred_element_type=F32
        )
        pb[m, :, core, :, k * WIDE : k * WIDE + UNITS] = value.astype(BF16).reshape(
            NY, NX * CAP, UNITS
        )

    def down_product(m, core):
        rows = hb[m, :, core].reshape(NY * NX * CAP, WIDE)[:, :UNITS]
        part = jnp.dot(rows, down_w[m], preferred_element_type=F32)
        yo[m, :, core] = part.astype(BF16).reshape(NY, NX, CAP, 512)

    def middle(m):
        if m == 0:
            ready()
        at = {o: around(y, o, NY) for o in range(NY)}
        core = []
        for k in (0, 1):
            partial(m, 1 - c, k)
            side = pl.ds(k * WIDE, WIDE)
            core.append(wire(pb.at[m, :, 1 - c, :, side], cr.at[m, :, :, side], other))
        yield
        partial(m, c, 0)
        partial(m, c, 1)
        landed(core)
        pb[m, at[2], c] = pb[m, at[2], c] + cr[m, at[2]]
        moving = [
            wire(pb.at[m, at[2], c, :, pl.ds(0, WIDE)], ya.at[m, 0], y_right),
            wire(pb.at[m, at[2], c, :, pl.ds(WIDE, WIDE)], ya.at[m, 1], y_left),
        ]
        for o in (1, 3):
            pb[m, at[o], c] = pb[m, at[o], c] + cr[m, at[o]]
        yield
        landed(moving)
        pb[m, at[1], c, :, 0:WIDE] = pb[m, at[1], c, :, 0:WIDE] + ya[m, 0]
        moving = [wire(pb.at[m, at[1], c], yb.at[m, 0], y_right)]
        pb[m, at[3], c, :, WIDE:] = pb[m, at[3], c, :, WIDE:] + ya[m, 1]
        moving.append(wire(pb.at[m, at[3], c], yb.at[m, 1], y_left))
        yield
        landed(moving)
        both = (
            pb[m, y, c].astype(F32)
            + cr[m, y].astype(F32)
            + yb[m, 0].astype(F32)
            + yb[m, 1].astype(F32)
        )
        gate, up = both[:, :WIDE], both[:, WIDE:]
        hb[m, y, c] = (gate / (1.0 + jnp.exp(-gate)) * up).astype(BF16)

        def pass_on(o, to, rows=None):
            ref = hb.at[m, at[o], c] if rows is None else hb.at[m, at[o], c, pl.ds(rows, 96)]
            return wire(ref, ref, to)

        moving = [pass_on(0, y_right), pass_on(0, y_left)]
        across = [pass_on(0, other)]
        yield
        landed(moving)
        moving = [pass_on(3, y_right, 0), pass_on(1, y_left, 96)]
        across += [pass_on(3, other), pass_on(1, other)]
        yield
        landed(moving)
        across.append(pass_on(2, other))
        down_product(m, c)
        landed(across)
        down_product(m, 1 - c)

    def scatter_first(m):
        def put_z(value):
            yo[(m, *plane(z), slice(None), slice(None), slice(0, HALF))] = value.astype(BF16)

        def put(value):
            fin[m, :, 0:HALF] = value.astype(BF16)

        yield from scatter(
            wire, "z", NZ, z,
            lambda j, p: yo.at[(m, *plane(j), slice(None), slice(None), cut(0, p))],
            lambda k, p: za.at[m, k, :, :, cut(0, p)],
            put_z,
        )
        yield from scatter_at_once(
            wire, "x", NX, x,
            lambda j, p: yo.at[(m, *plane(z), j, slice(None), cut(0, p))],
            lambda k, p: xa.at[m, k, :, cut(0, p)],
            put,
        )

    def scatter_second(m):
        def put_x(value):
            yo[m, :, :, x, :, HALF : 2 * HALF] = value.astype(BF16)

        def put(value):
            fin[m, :, HALF : 2 * HALF] = value.astype(BF16)

        yield from scatter(
            wire, "x", NX, x,
            lambda j, p: yo.at[m, :, :, j, :, cut(HALF, p)],
            lambda k, p: xc.at[m, k, :, :, :, cut(0, p)],
            put_x,
        )
        way = scatter_at_once if m == MODS - 1 else scatter
        yield from way(
            wire, "z", NZ, z,
            lambda j, p: yo.at[(m, *plane(j), x, slice(None), cut(HALF, p))],
            lambda k, p: zc.at[m, k, :, cut(0, p)],
            put,
        )

    def chain(m):
        for _ in range(STAGGER * m):
            yield
        yield from together(gather_first(m), gather_second(m))
        yield from middle(m)
        yield from together(scatter_first(m), scatter_second(m))

    for _ in together(*[chain(m) for m in range(MODS)]):
        pass


def layer_kernel(*args):
    refs, args = args[:7], args[7:]
    (gate_ref, up_ref, down_ref, out_ref), args = args[:4], args[4:]
    (send, recv, local), args = args[:3], args[3:]
    (xb, stream, gate_w, up_w, down_w), args = args[:5], args[5:]
    attend_scratch, ffn_scratch = args[:16], args[16:]
    here = z, x, y, c = tuple(lax.axis_index(a) for a in ("z", "x", "y", "c"))
    peers = [around(2 * y + c, o, 8) for o in range(1, 8)]
    fetched = []

    def fetch(src, dst):
        copy = pltpu.make_async_copy(src, dst, local.at[len(fetched)])
        fetched.append(copy)
        copy.start()
        return copy

    greet(
        [{"x": around(x, o, NX)} for o in range(1, NX)]
        + [{"z": around(z, o, NZ)} for o in range(1, NZ)]
        + [{"y": lax.div(p, 2), "c": lax.rem(p, 2)} for p in peers]
    )
    wire = Wire(send, recv)
    tags, stream_ref, fin = attend_scratch[14], stream, ffn_scratch[-1]
    loads = []

    def ready():
        for copy in loads:
            copy.wait()

    def begin():
        for src, dst in ((gate_ref, gate_w), (up_ref, up_w), (down_ref, down_w)):
            loads.append(fetch(src, dst))

    begin()
    attend(wire, here, refs, fetch, xb, stream_ref, attend_scratch)
    feed_forward(wire, here, (gate_w, up_w, down_w, ready), xb, ffn_scratch)

    tag_row = tags[...]
    tag_col = to_column(tag_row)
    rank = jnp.sum(
        jnp.where(
            (tag_col == tag_row) & (iota((ROWS, ROWS), 1) < iota((ROWS, ROWS), 0)), 1.0, 0.0
        ),
        axis=1,
        keepdims=True,
    ).astype(jnp.int32)
    slot = iota((ROWS, CAP), 1)
    result = stream[...]
    for m in range(MODS):
        placing = jnp.where((tag_col == m) & (rank == slot), 1.0, 0.0).astype(BF16)
        result = result + jnp.dot(placing, fin[m], preferred_element_type=F32)
    out_ref[...] = result.astype(BF16)
    wire.drain()


def on_device(resid, queries, keys, values, doc_ids, modality, norm_gain, gate_w, up_w, down_w):
    block = (NX, ROWS, DH)
    i32 = jnp.int32
    shapes = [
        ((MODS, NY, 2, NX, CAP, 512), BF16),
        ((ROWS, 512), F32),
        ((MODS, UNITS, 512), BF16),
        ((MODS, UNITS, 512), BF16),
        ((MODS, UNITS, 512), BF16),
        (block, BF16),
        ((BACK + 1, *block), BF16),
        ((BACK + 1, *block), BF16),
        ((BACK - 1, TURNED, ROWS, DH), BF16),
        ((BACK - 1, TURNED, ROWS, DH), BF16),
        ((BACK + 1, NX, 1, ROWS), i32),
        ((NX, ROWS, 1), i32),
        ((NX, ROWS, 1), F32),
        ((NX, ROWS, 1), F32),
        (block, F32),
        (block, BF16),
        (block, BF16),
        ((8, 1, ROWS), F32),
        ((ROWS, 512), BF16),
        ((1, ROWS), i32),
        ((MODS, 512), F32),
        ((MODS, NY, 2, NX * CAP, 2 * WIDE), BF16),
        ((MODS, NY, NX * CAP, 2 * WIDE), BF16),
        ((MODS, 2, NX * CAP, WIDE), BF16),
        ((MODS, 2, NX * CAP, 2 * WIDE), BF16),
        ((MODS, NY, 2, NX * CAP, WIDE), BF16),
        ((MODS, NY, 2, NX, CAP, 512), BF16),
        ((MODS, NZ, NX, CAP, HALF), BF16),
        ((MODS, NX, CAP, HALF), BF16),
        ((MODS, NZ, CAP, HALF), BF16),
        ((MODS, NX, NY, 2, CAP, HALF), BF16),
        ((MODS, CAP, 512), BF16),
    ]
    dma = pltpu.SemaphoreType.DMA
    return pl.pallas_call(
        layer_kernel,
        out_shape=jax.ShapeDtypeStruct((ROWS, 512), BF16),
        in_specs=[pl.BlockSpec(memory_space=pl.ANY)] * 10,
        out_specs=pl.BlockSpec(memory_space=pltpu.VMEM),
        scratch_shapes=[dma((280,)), dma((280,)), dma((12,))]
        + [pltpu.VMEM(shape, kind) for shape, kind in shapes],
        compiler_params=pltpu.CompilerParams(
            collective_id=0, has_side_effects=True, vmem_limit_bytes=60 << 20
        ),
        name="layer",
    )(
        queries,
        keys,
        values,
        resid,
        doc_ids.reshape(1, ROWS),
        modality.reshape(1, ROWS),
        norm_gain,
        gate_w.transpose(1, 2, 0),
        up_w.transpose(1, 2, 0),
        down_w,
    )


def solution(mesh):
    split = Mesh(mesh.devices.reshape(NZ, NX, NY, 2), ("z", "x", "y", "c"))
    placed = (
        P(SEQ, TENSOR),
        P(SEQ, TENSOR),
        P(SEQ, TENSOR),
        P(SEQ, TENSOR),
        P(SEQ),
        P(SEQ),
        P(None, TENSOR),
        P(TENSOR, None, SEQ),
        P(TENSOR, None, SEQ),
        P(None, SEQ, TENSOR),
    )
    return jax.shard_map(
        on_device, mesh=split, in_specs=placed, out_specs=P(SEQ, TENSOR), check_vma=False
    )
```

```python
import math

import jax
import jax.numpy as jnp
from jax import lax
from jax.experimental import pallas as pl
from jax.experimental.pallas import tpu as pltpu
from jax.sharding import Mesh
from jax.sharding import PartitionSpec as P

D = 4096
DH = 128
MODS = 3
CAP = 48
ROWS = 128
NZ, NX, NY = 8, 4, 4
BACK = 4
TURNED = 3
UNITS, WIDE = 344, 384
HALF = 256
PAIR = 2
WHOLE = 1
ORDER = (
    2, 12, 12, 2, 1, 12, 2, 1, 12, 2, 1, 0, 12, 2, 1, 0, 2, 7, 8, 7, 12, 1, 8, 0,
    1, 7, 12, 6, 5, 0, 8, 6, 5, 7, 0, 8, 6, 0, 3, 5, 4, 7, 3, 4, 8, 6, 5, 7,
    3, 4, 8, 11, 6, 5, 3, 11, 4, 6, 5, 11, 3, 13, 4, 10, 3, 11, 4, 9, 13, 10, 11, 9,
    10, 13, 9, 11, 10, 13, 9, 10, 13, 9, 13, 10, 13, 9,
)
SEQ = ("z", "x")
TENSOR = ("y", "c")
MESH = pl.DeviceIdType.MESH
F32, BF16 = jnp.float32, jnp.bfloat16


def around(i, by, n):
    return lax.rem(i + (by % n), n)


class Wire:
    def __init__(self, send, recv):
        self.send, self.recv, self.copies = send, recv, []

    def __call__(self, src, dst, to):
        k = len(self.copies)
        copy = pltpu.make_async_remote_copy(
            src_ref=src,
            dst_ref=dst,
            send_sem=self.send.at[k],
            recv_sem=self.recv.at[k],
            device_id=to,
            device_id_type=MESH,
        )
        self.copies.append(copy)
        copy.start()
        return copy

    def drain(self):
        for copy in self.copies:
            copy.wait_send()


def landed(copies):
    for copy in copies:
        copy.wait_recv()


def greet(partners):
    barrier = pltpu.get_barrier_semaphore()
    for partner in partners:
        pl.semaphore_signal(barrier, inc=1, device_id=partner, device_id_type=MESH)
    pl.semaphore_wait(barrier, len(partners))


def iota(shape, dim):
    return lax.broadcasted_iota(jnp.int32, shape, dim)


def eye():
    return iota((ROWS, ROWS), 0) == iota((ROWS, ROWS), 1)


def to_column(row):
    return jnp.sum(jnp.where(eye(), row, jnp.zeros_like(row)), axis=1, keepdims=True)


def to_row(column):
    return jnp.sum(jnp.where(eye(), column, jnp.zeros_like(column)), axis=0, keepdims=True)


def attend(wire, here, refs, fetch, lend, xb, xf, stream, scratch):
    z, x, y, c = here
    q_ref, k_ref, v_ref, resid_ref, docs_ref, tags_ref, gain_ref = refs
    qb, kb, vb, kr, vr, db, dcol, top, total, acc, ab, att, sqb, resid, tags, gain = scratch
    t = 2 * y + c
    up, down = {"z": around(z, 1, NZ)}, {"z": around(z, -1, NZ)}
    order = (2, 1, 3, 0)
    at = {o: around(x, o, NX) for o in order}

    def cols(p):
        return pl.ds(pl.multiple_of(p * DH, DH), DH)

    local = [
        fetch(k_ref.at[:, cols(x)], kb.at[0, x]),
        fetch(v_ref.at[:, cols(x)], vb.at[0, x]),
        fetch(docs_ref, db.at[0, x]),
        fetch(q_ref.at[:, cols(x)], qb.at[x]),
        fetch(tags_ref, tags),
        fetch(gain_ref, gain),
        fetch(resid_ref, resid),
    ]
    coming = {"k": [], "v": [], "q": []}
    for o in order[:3]:
        coming["k"].append(wire(k_ref.at[:, cols(at[o])], kb.at[0, x], {"x": at[o]}))
    for o in order[:3]:
        coming["v"].append(wire(v_ref.at[:, cols(at[o])], vb.at[0, x], {"x": at[o]}))
    for o in order[:3]:
        coming["q"].append(wire(docs_ref, db.at[0, x], {"x": at[o]}))
        coming["q"].append(wire(q_ref.at[:, cols(at[o])], qb.at[x], {"x": at[o]}))
    lend()

    near = pl.ds(0, TURNED)
    rest = pl.ds(TURNED, NX - TURNED)

    def forward(b, r, d):
        if d == BACK:
            return []
        if d + 1 < BACK:
            moving = [wire(b.at[d], b.at[d + 1], up)]
        else:
            moving = [wire(b.at[d, rest], b.at[d + 1, rest], up)]
        source = b.at[0, near] if d == 0 else r.at[d - 1]
        target = b.at[BACK, near] if d + 1 == BACK else r.at[d]
        return moving + [wire(source, target, down)]

    local[0].wait()
    landed(coming["k"])
    moving_k = forward(kb, kr, 0)
    local[1].wait()
    landed(coming["v"])
    moving_v = forward(vb, vr, 0)
    local[2].wait()
    local[3].wait()
    landed(coming["q"])
    moving_d = [wire(db.at[0], db.at[1], up)]
    for o in order:
        dcol[at[o]] = to_column(db[0, at[o]])
    factor = math.log2(math.e) / math.sqrt(DH)
    returned = []

    def block(d, o):
        j = at[o]
        keys = kb[d].reshape(NX * ROWS, DH)
        vals = vb[d].reshape(NX * ROWS, DH)
        key_docs = jnp.concatenate([db[d, i] for i in range(NX)], axis=1)
        score = lax.dot_general(
            qb[j], keys, (((1,), (1,)), ((), ())), preferred_element_type=F32
        )
        if d == 0:
            allowed = (iota(score.shape, 1) <= j * ROWS + iota(score.shape, 0)) & (
                key_docs == dcol[j]
            )
        else:
            allowed = jnp.where(z < d, -1, key_docs) == dcol[j]
        score = jnp.where(allowed, score, -1e30)
        high = jnp.max(score, axis=1, keepdims=True)
        if d > 0:
            old = top[j]
            high = jnp.maximum(high, old)
        power = jnp.exp2((score - high) * factor)
        add = jnp.sum(power, axis=1, keepdims=True)
        blend = jnp.dot(power.astype(BF16), vals, preferred_element_type=F32)
        if d > 0:
            fade = jnp.exp2((old - high) * factor)
            add = add + fade * total[j]
            blend = blend + fade * acc[j]
        if d < BACK:
            top[j] = high
            total[j] = add
            acc[j] = blend
            return
        result = (blend / add).astype(BF16)
        if o == 0:
            att[x] = result
        else:
            ab[j] = result
            returned.append(wire(ab.at[j], att.at[x], {"x": j}))

    for d in range(1, BACK + 1):
        landed(moving_k)
        moving_k = forward(kb, kr, d)
        block(d - 1, 2)
        block(d - 1, 1)
        landed(moving_v)
        moving_v = forward(vb, vr, d)
        landed(moving_d)
        if d < BACK:
            moving_d = [wire(db.at[d], db.at[d + 1], up)]
        block(d - 1, 3)
        block(d - 1, 0)
    for o in order:
        block(BACK, o)

    for copy in local[4:]:
        copy.wait()
    tag_row = tags[...]
    tag_col = to_column(tag_row)
    rank = jnp.sum(
        jnp.where(
            (tag_col == tag_row) & (iota((ROWS, ROWS), 0) < iota((ROWS, ROWS), 1)), 1.0, 0.0
        ),
        axis=0,
        keepdims=True,
    ).astype(jnp.int32)
    slot = iota((CAP, ROWS), 0)
    landed(returned)
    flow = resid[...].astype(F32) + jnp.concatenate(
        [att[i].astype(F32) for i in range(NX)], axis=1
    )
    stream[...] = flow
    sqb[t] = to_row(jnp.sum(flow * flow, axis=1, keepdims=True))
    peers = [around(t, o, 8) for o in range(1, 8)]
    coming = [wire(sqb.at[t], sqb.at[t], {"y": lax.div(p, 2), "c": lax.rem(p, 2)}) for p in peers]
    gains = jnp.where(
        tag_col == 0, gain[0:1, :], jnp.where(tag_col == 1, gain[1:2, :], gain[2:3, :])
    )
    landed(coming)
    inv = to_column(lax.rsqrt(jnp.sum(sqb[...], axis=0) / D + 1e-5))
    normed = (flow * inv * gains).astype(BF16)
    for m in range(MODS):
        placing = jnp.where((tag_row == m) & (rank == slot), 1.0, 0.0).astype(BF16)
        rows = jnp.dot(placing, normed, preferred_element_type=F32).astype(BF16)
        if m == WHOLE:
            xf[lax.div(z, 2), lax.rem(z, 2), x] = rows
        else:
            xb[m, lax.div(z, 2), lax.rem(z, 2), lax.div(x, 2)] = rows


def gather(wire, axis, n, me, view):
    half = n // 2
    for s in range(1, half + 1):
        last = s == half
        right = view(around(me, 1 - s, n), 0 if last else None)
        left = view(around(me, s - 1, n), 1 if last else None)
        moving = [
            wire(right, right, {axis: around(me, 1, n)}),
            wire(left, left, {axis: around(me, -1, n)}),
        ]
        yield
        landed(moving)


def scatter(wire, axis, n, me, view, landing):
    half = n // 2
    for s in range(1, half + 1):
        far = half - s + 1
        part = (0, 1) if s == 1 else (None, None)
        to = (around(me, far, n), around(me, -far, n))
        if s > 1:
            before = (0, 1) if s == 2 else (None, None)
            for side in (0, 1):
                total = view(to[side], before[side])
                total[...] = total[...] + landing(side * half + s - 2, before[side])[...]
        moving = [
            wire(
                view(to[side], part[side]),
                landing(side * half + s - 1, part[side]),
                {axis: around(me, by, n)},
            )
            for side, by in ((0, 1), (1, -1))
        ]
        yield
        landed(moving)
    total = view(me, None)
    total[...] = (
        total[...].astype(F32)
        + landing(half - 1, None)[...].astype(F32)
        + landing(n - 1, None)[...].astype(F32)
    ).astype(BF16)


def cut(part):
    return pl.ds(0, 512) if part is None else pl.ds(HALF * part, HALF)


def side_cut(base, part):
    return pl.ds(base, HALF) if part is None else pl.ds(base + 128 * part, 128)


def feed_forward(wire, here, weights, xb, xf, scratch):
    z, x, y, c = here
    pb, cr, ya, yb, hb, yo, za, xa, yf, zf, xs, zs, xf2, fin = scratch
    gate_w, up_w, down_w, ready = weights
    k = lax.div(x, 2)
    twin = {"x": around(x, 2, NX)}
    other = {"c": 1 - c}
    y_right, y_left = {"y": around(y, 1, NY)}, {"y": around(y, -1, NY)}
    rows_of = PAIR * CAP

    def plane(j):
        return lax.div(j, 2), lax.rem(j, 2)

    def rows_in(m):
        mine = xb.at[(m, *plane(z), k)]
        moving = [wire(mine, mine, twin)]
        yield
        landed(moving)
        yield from gather(
            wire, "z", NZ, z,
            lambda j, p: xb.at[(m, *plane(j), slice(None), slice(None), cut(p))],
        )

    def whole_first():
        row = plane(z)
        mine = xf.at[(*row, x, slice(None), pl.ds(0, HALF))]
        moving = [wire(mine, mine, {"x": around(x, o, NX)}) for o in (2, 1, 3)]
        yield
        landed(moving)
        yield from gather(
            wire, "z", NZ, z,
            lambda j, p: xf.at[(*plane(j), slice(None), slice(None), side_cut(0, p))],
        )

    def whole_second():
        yield from gather(
            wire, "z", NZ, z, lambda j, p: xf.at[(*plane(j), x, slice(None), side_cut(HALF, p))]
        )
        yield from gather(wire, "x", NX, x, lambda j, p: xf.at[:, :, j, :, side_cut(HALF, p)])

    def partial(m, e, core, side):
        if m == WHOLE:
            rows = xf[:, core, PAIR * e : PAIR * (e + 1)]
            w = (gate_w, up_w)[side][0, m]
        else:
            rows = xb[m, :, core]
            w = (gate_w, up_w)[side][e, m]
        rows = rows.reshape(NY * rows_of, 512)
        value = lax.dot_general(
            rows, w, (((1,), (1,)), ((), ())), preferred_element_type=F32
        )
        pb[m, e, :, core, :, side * WIDE : side * WIDE + UNITS] = value.astype(BF16).reshape(
            NY, rows_of, UNITS
        )

    def hidden(m, e):
        ready(m, e)
        at = {o: around(y, o, NY) for o in range(NY)}
        core = []
        for side in (0, 1):
            partial(m, e, 1 - c, side)
            cols = pl.ds(side * WIDE, WIDE)
            core.append(wire(pb.at[m, e, :, 1 - c, :, cols], cr.at[m, e, :, :, cols], other))
        yield
        partial(m, e, c, 0)
        partial(m, e, c, 1)
        landed(core)
        pb[m, e, at[2], c] = pb[m, e, at[2], c] + cr[m, e, at[2]]
        moving = [
            wire(pb.at[m, e, at[2], c, :, pl.ds(0, WIDE)], ya.at[m, e, 0], y_right),
            wire(pb.at[m, e, at[2], c, :, pl.ds(WIDE, WIDE)], ya.at[m, e, 1], y_left),
        ]
        for o in (1, 3):
            pb[m, e, at[o], c] = pb[m, e, at[o], c] + cr[m, e, at[o]]
        yield
        landed(moving)
        pb[m, e, at[1], c, :, 0:WIDE] = pb[m, e, at[1], c, :, 0:WIDE] + ya[m, e, 0]
        moving = [wire(pb.at[m, e, at[1], c], yb.at[m, e, 0], y_right)]
        pb[m, e, at[3], c, :, WIDE:] = pb[m, e, at[3], c, :, WIDE:] + ya[m, e, 1]
        moving.append(wire(pb.at[m, e, at[3], c], yb.at[m, e, 1], y_left))
        yield
        landed(moving)
        both = (
            pb[m, e, y, c].astype(F32)
            + cr[m, e, y].astype(F32)
            + yb[m, e, 0].astype(F32)
            + yb[m, e, 1].astype(F32)
        )
        gate, up = both[:, :WIDE], both[:, WIDE:]
        hb[m, e, y, c] = (gate / (1.0 + jnp.exp(-gate)) * up).astype(BF16)

        def pass_on(o, to, first=None):
            ref = hb.at[m, e, at[o], c]
            if first is not None:
                ref = hb.at[m, e, at[o], c, pl.ds(first, CAP)]
            return wire(ref, ref, to)

        moving = [pass_on(0, y_right), pass_on(0, y_left)]
        across = [pass_on(0, other)]
        yield
        landed(moving)
        moving = [pass_on(3, y_right, 0), pass_on(1, y_left, CAP)]
        across += [pass_on(3, other), pass_on(1, other)]
        yield
        landed(moving)
        across.append(pass_on(2, other))
        landed(across)

    def sums_out(m):
        for core in (0, 1):
            part = jnp.zeros((NY * rows_of, 512), F32)
            for e in (0, 1):
                rows = hb[m, e, :, core].reshape(NY * rows_of, WIDE)[:, :UNITS]
                part = part + jnp.dot(rows, down_w[e, m], preferred_element_type=F32)
            yo[m, :, core] = part.astype(BF16).reshape(NY, PAIR, CAP, 512)
        yield from scatter(
            wire, "z", NZ, z,
            lambda j, p: yo.at[(m, *plane(j), slice(None), slice(None), cut(p))],
            lambda n, p: za.at[m, n, :, :, cut(p)],
        )
        moving = [wire(yo.at[(m, *plane(z), 1 - k)], xa.at[m], twin)]
        yield
        landed(moving)
        fin[m] = yo[(m, *plane(z), k)] + xa[m]

    made = []

    def products():
        if made:
            return
        made.append(True)
        for core in (0, 1):
            for e in (0, 1):
                rows = hb[WHOLE, e, :, core].reshape(NY * rows_of, WIDE)[:, :UNITS]
                part = jnp.dot(rows, down_w[0, WHOLE], preferred_element_type=F32)
                yf[:, core, PAIR * e : PAIR * (e + 1)] = part.astype(BF16).reshape(
                    NY, PAIR, CAP, 512
                )

    def whole_out_first():
        products()
        yield from scatter(
            wire, "z", NZ, z,
            lambda j, p: yf.at[(*plane(j), slice(None), slice(None), side_cut(0, p))],
            lambda n, p: zf.at[n, :, :, side_cut(0, p)],
        )
        moving = []
        for o in (2, 1, 3):
            to = around(x, o, NX)
            source = yf.at[(*plane(z), to, slice(None), pl.ds(0, HALF))]
            moving.append(wire(source, xs.at[o], {"x": to}))
        yield
        landed(moving)
        total = yf[(*plane(z), x, slice(None), slice(0, HALF))].astype(F32)
        for o in (1, 2, 3):
            total = total + xs[o].astype(F32)
        fin[WHOLE, :, 0:HALF] = total.astype(BF16)

    def whole_out_second():
        products()
        yield from scatter(
            wire, "x", NX, x,
            lambda j, p: yf.at[:, :, j, :, side_cut(HALF, p)],
            lambda n, p: xf2.at[n, :, :, :, side_cut(0, p)],
        )
        yield from scatter(
            wire, "z", NZ, z,
            lambda j, p: yf.at[(*plane(j), x, slice(None), side_cut(HALF, p))],
            lambda n, p: zs.at[n, :, side_cut(0, p)],
        )
        fin[WHOLE, :, HALF : 2 * HALF] = yf[(*plane(z), x, slice(None), slice(HALF, 2 * HALF))]

    work = [rows_in(0), whole_first(), rows_in(2)]
    work += [hidden(m, e) for m in range(MODS) for e in (0, 1)]
    work += [sums_out(0), whole_out_first(), sums_out(2), whole_second(), whole_out_second()]
    for n in ORDER:
        next(work[n], None)
    for process in work:
        for _ in process:
            pass


def layer_kernel(*args):
    refs, args = args[:7], args[7:]
    (gate_ref, up_ref, down_ref, out_ref), args = args[:4], args[4:]
    (send, recv, local), args = args[:3], args[3:]
    (xb, xf, stream, gate_w, up_w, down_w), args = args[:6], args[6:]
    attend_scratch, ffn_scratch = args[:16], args[16:]
    here = z, x, y, c = tuple(lax.axis_index(a) for a in ("z", "x", "y", "c"))
    peers = [around(2 * y + c, o, 8) for o in range(1, 8)]
    fetched = []

    def fetch(src, dst):
        copy = pltpu.make_async_copy(src, dst, local.at[len(fetched)])
        fetched.append(copy)
        copy.start()
        return copy

    greet(
        [{"x": around(x, o, NX)} for o in range(1, NX)]
        + [{"z": around(z, o, NZ)} for o in range(1, NZ)]
        + [{"y": lax.div(p, 2), "c": lax.rem(p, 2)} for p in peers]
    )
    wire = Wire(send, recv)
    tags, stream_ref, fin = attend_scratch[14], stream, ffn_scratch[-1]
    right, left = {"x": around(x, 1, NX)}, {"x": around(x, -1, NX)}
    weights = ((gate_ref, gate_w), (up_ref, up_w), (down_ref, down_w))
    own, lent = [], {}

    def lend():
        for m in (0, 2):
            to = left if m == 2 else right
            lent[m] = [wire(src.at[m], dst.at[1, m], to) for src, dst in weights]
        for src, dst in weights:
            own.append(fetch(src, dst.at[0]))

    def ready(m, e):
        if e == 1 and m != WHOLE:
            landed(lent[m])
        while own:
            own.pop().wait()

    attend(wire, here, refs, fetch, lend, xb, xf, stream_ref, attend_scratch)
    feed_forward(wire, here, (gate_w, up_w, down_w, ready), xb, xf, ffn_scratch)

    tag_row = tags[...]
    tag_col = to_column(tag_row)
    rank = jnp.sum(
        jnp.where(
            (tag_col == tag_row) & (iota((ROWS, ROWS), 1) < iota((ROWS, ROWS), 0)), 1.0, 0.0
        ),
        axis=1,
        keepdims=True,
    ).astype(jnp.int32)
    slot = iota((ROWS, CAP), 1)
    result = stream[...]
    for m in range(MODS):
        placing = jnp.where((tag_col == m) & (rank == slot), 1.0, 0.0).astype(BF16)
        result = result + jnp.dot(placing, fin[m], preferred_element_type=F32)
    out_ref[...] = result.astype(BF16)
    wire.drain()


def on_device(resid, queries, keys, values, doc_ids, modality, norm_gain, gate_w, up_w, down_w):
    block = (NX, ROWS, DH)
    i32 = jnp.int32
    shapes = [
        ((MODS, NY, 2, PAIR, CAP, 512), BF16),
        ((NY, 2, NX, CAP, 512), BF16),
        ((ROWS, 512), F32),
        ((2, MODS, UNITS, 512), BF16),
        ((2, MODS, UNITS, 512), BF16),
        ((2, MODS, UNITS, 512), BF16),
        (block, BF16),
        ((BACK + 1, *block), BF16),
        ((BACK + 1, *block), BF16),
        ((BACK - 1, TURNED, ROWS, DH), BF16),
        ((BACK - 1, TURNED, ROWS, DH), BF16),
        ((BACK + 1, NX, 1, ROWS), i32),
        ((NX, ROWS, 1), i32),
        ((NX, ROWS, 1), F32),
        ((NX, ROWS, 1), F32),
        (block, F32),
        (block, BF16),
        (block, BF16),
        ((8, 1, ROWS), F32),
        ((ROWS, 512), BF16),
        ((1, ROWS), i32),
        ((MODS, 512), F32),
        ((MODS, 2, NY, 2, PAIR * CAP, 2 * WIDE), BF16),
        ((MODS, 2, NY, PAIR * CAP, 2 * WIDE), BF16),
        ((MODS, 2, 2, PAIR * CAP, WIDE), BF16),
        ((MODS, 2, 2, PAIR * CAP, 2 * WIDE), BF16),
        ((MODS, 2, NY, 2, PAIR * CAP, WIDE), BF16),
        ((MODS, NY, 2, PAIR, CAP, 512), BF16),
        ((MODS, NZ, PAIR, CAP, 512), BF16),
        ((MODS, CAP, 512), BF16),
        ((NY, 2, NX, CAP, 512), BF16),
        ((NZ, NX, CAP, HALF), BF16),
        ((NX, CAP, HALF), BF16),
        ((NZ, CAP, HALF), BF16),
        ((NX, NY, 2, CAP, HALF), BF16),
        ((MODS, CAP, 512), BF16),
    ]
    dma = pltpu.SemaphoreType.DMA
    return pl.pallas_call(
        layer_kernel,
        out_shape=jax.ShapeDtypeStruct((ROWS, 512), BF16),
        in_specs=[pl.BlockSpec(memory_space=pl.ANY)] * 10,
        out_specs=pl.BlockSpec(memory_space=pltpu.VMEM),
        scratch_shapes=[dma((280,)), dma((280,)), dma((12,))]
        + [pltpu.VMEM(shape, kind) for shape, kind in shapes],
        compiler_params=pltpu.CompilerParams(
            collective_id=0, has_side_effects=True, vmem_limit_bytes=60 << 20
        ),
        name="layer",
    )(
        queries,
        keys,
        values,
        resid,
        doc_ids.reshape(1, ROWS),
        modality.reshape(1, ROWS),
        norm_gain,
        gate_w.transpose(1, 2, 0),
        up_w.transpose(1, 2, 0),
        down_w,
    )


def solution(mesh):
    split = Mesh(mesh.devices.reshape(NZ, NX, NY, 2), ("z", "x", "y", "c"))
    placed = (
        P(SEQ, TENSOR),
        P(SEQ, TENSOR),
        P(SEQ, TENSOR),
        P(SEQ, TENSOR),
        P(SEQ),
        P(SEQ),
        P(None, TENSOR),
        P(TENSOR, None, SEQ),
        P(TENSOR, None, SEQ),
        P(None, SEQ, TENSOR),
    )
    return jax.shard_map(
        on_device, mesh=split, in_specs=placed, out_specs=P(SEQ, TENSOR), check_vma=False
    )
```

```python
import math

import jax
import jax.numpy as jnp
from jax import lax
from jax.experimental import pallas as pl
from jax.experimental.pallas import tpu as pltpu
from jax.sharding import Mesh
from jax.sharding import PartitionSpec as P

D = 4096
DH = 128
MODS = 3
CAP = 48
ROWS = 128
NZ, NX, NY = 8, 4, 4
BACK = 4
TURNED = 3
UNITS, WIDE = 344, 384
HALF = 256
PAIR = 2
WHOLE = 1
ORDER = (
    15, 2, 12, 15, 12, 2, 15, 12, 2, 1, 15, 12, 2, 15, 12, 1, 2, 14, 1, 2, 0, 15, 7, 8,
    14, 7, 8, 1, 12, 0, 14, 7, 8, 1, 12, 0, 14, 7, 1, 5, 6, 0, 14, 8, 5, 7, 6, 0,
    8, 5, 0, 7, 14, 4, 6, 8, 17, 5, 11, 4, 3, 6, 11, 5, 3, 4, 17, 11, 6, 5, 3, 17,
    11, 4, 17, 6, 10, 11, 17, 3, 13, 4, 10, 11, 17, 3, 13, 4, 10, 3, 16, 9, 13, 10, 9, 13,
    10, 16, 9, 13, 16, 10, 9, 13, 16, 9, 13, 16, 9, 16,
)
SEQ = ("z", "x")
TENSOR = ("y", "c")
MESH = pl.DeviceIdType.MESH
F32, BF16 = jnp.float32, jnp.bfloat16


def around(i, by, n):
    return lax.rem(i + (by % n), n)


class Wire:
    def __init__(self, send, recv):
        self.send, self.recv, self.copies = send, recv, []

    def __call__(self, src, dst, to):
        k = len(self.copies)
        copy = pltpu.make_async_remote_copy(
            src_ref=src,
            dst_ref=dst,
            send_sem=self.send.at[k],
            recv_sem=self.recv.at[k],
            device_id=to,
            device_id_type=MESH,
        )
        self.copies.append(copy)
        copy.start()
        return copy

    def drain(self):
        for copy in self.copies:
            copy.wait_send()


def landed(copies):
    for copy in copies:
        copy.wait_recv()


def greet(partners):
    barrier = pltpu.get_barrier_semaphore()
    for partner in partners:
        pl.semaphore_signal(barrier, inc=1, device_id=partner, device_id_type=MESH)
    pl.semaphore_wait(barrier, len(partners))


def iota(shape, dim):
    return lax.broadcasted_iota(jnp.int32, shape, dim)


def eye():
    return iota((ROWS, ROWS), 0) == iota((ROWS, ROWS), 1)


def to_column(row):
    return jnp.sum(jnp.where(eye(), row, jnp.zeros_like(row)), axis=1, keepdims=True)


def to_row(column):
    return jnp.sum(jnp.where(eye(), column, jnp.zeros_like(column)), axis=0, keepdims=True)


def attend(wire, here, refs, fetch, lend, xb, xf, stream, scratch):
    z, x, y, c = here
    q_ref, k_ref, v_ref, resid_ref, docs_ref, tags_ref, gain_ref = refs
    qb, kb, vb, kr, vr, db, dcol, top, total, acc, ab, att, sqb, resid, tags, gain = scratch
    t = 2 * y + c
    up, down = {"z": around(z, 1, NZ)}, {"z": around(z, -1, NZ)}
    order = (2, 1, 3, 0)
    at = {o: around(x, o, NX) for o in order}

    def cols(p):
        return pl.ds(pl.multiple_of(p * DH, DH), DH)

    local = [
        fetch(k_ref.at[:, cols(x)], kb.at[0, x]),
        fetch(v_ref.at[:, cols(x)], vb.at[0, x]),
        fetch(docs_ref, db.at[0, x]),
        fetch(q_ref.at[:, cols(x)], qb.at[x]),
        fetch(tags_ref, tags),
        fetch(gain_ref, gain),
        fetch(resid_ref, resid),
    ]
    sides = ((k_ref, kb, kr), (v_ref, vb, vr))
    coming, asked = {}, []
    for o in order[:3]:
        coming[o] = [wire(ref.at[:, cols(at[o])], b.at[0, x], {"x": at[o]}) for ref, b, _ in sides]
    slot = {o: around(x, -o, NX) for o in order}
    rising = {0: [wire(ref.at[:, cols(x)], b.at[1, x], up) for ref, b, _ in sides]}
    falling = {}
    for o in order[:3]:
        asked.append(wire(docs_ref, db.at[0, x], {"x": at[o]}))
        asked.append(wire(q_ref.at[:, cols(at[o])], qb.at[x], {"x": at[o]}))
    lend()

    for o in order[:3]:
        rising[o], falling[o] = [], []
        for copy, (_, b, r) in zip(coming[o], sides):
            copy.wait_recv()
            rising[o].append(wire(b.at[0, slot[o]], b.at[1, slot[o]], up))
            falling[o].append(wire(b.at[0, slot[o]], r.at[0, o - 1], down))

    def pass_on(d, o):
        came, fell = rising.pop(o, []), falling.pop(o, [])
        landed(came + fell)
        if d == BACK:
            return
        rising[o], falling[o] = [], []
        for _, b, r in sides:
            if d + 1 < BACK or o == 0:
                rising[o].append(wire(b.at[d, slot[o]], b.at[d + 1, slot[o]], up))
            if o > 0:
                target = b.at[BACK, slot[o]] if d + 1 == BACK else r.at[d, o - 1]
                falling[o].append(wire(r.at[d - 1, o - 1], target, down))

    local[0].wait()
    local[1].wait()
    local[2].wait()
    local[3].wait()
    landed(asked)
    moving_d = [wire(db.at[0], db.at[1], up)]
    for o in order:
        dcol[at[o]] = to_column(db[0, at[o]])
    factor = math.log2(math.e) / math.sqrt(DH)
    returned = []

    def block(d, j, n):
        some, rows = pl.ds(j, n), n * ROWS
        keys = kb[d].reshape(NX * ROWS, DH)
        vals = vb[d].reshape(NX * ROWS, DH)
        key_docs = jnp.concatenate([db[d, i] for i in range(NX)], axis=1)
        score = lax.dot_general(
            qb[some].reshape(rows, DH), keys, (((1,), (1,)), ((), ())), preferred_element_type=F32
        )
        if d == 0:
            allowed = (iota(score.shape, 1) <= j * ROWS + iota(score.shape, 0)) & (
                key_docs == dcol[some].reshape(rows, 1)
            )
        else:
            allowed = jnp.where(z < d, -1, key_docs) == dcol[some].reshape(rows, 1)
        score = jnp.where(allowed, score, -1e30)
        high = jnp.max(score, axis=1, keepdims=True)
        if d > 0:
            old = top[some].reshape(rows, 1)
            high = jnp.maximum(high, old)
        power = jnp.exp2((score - high) * factor)
        add = jnp.sum(power, axis=1, keepdims=True)
        blend = jnp.dot(power.astype(BF16), vals, preferred_element_type=F32)
        if d > 0:
            fade = jnp.exp2((old - high) * factor)
            add = add + fade * total[some].reshape(rows, 1)
            blend = blend + fade * acc[some].reshape(rows, DH)
        if d < BACK:
            top[some] = high.reshape(n, ROWS, 1)
            total[some] = add.reshape(n, ROWS, 1)
            acc[some] = blend.reshape(n, ROWS, DH)
            return None
        return (blend / add).astype(BF16)

    for d in range(1, BACK + 1):
        pass_on(d, 0)
        pass_on(d, 2)
        block(d - 1, 0, 2)
        pass_on(d, 1)
        pass_on(d, 3)
        landed(moving_d)
        if d < BACK:
            moving_d = [wire(db.at[d], db.at[d + 1], up)]
        block(d - 1, 2, 2)
    for o in order[:3]:
        ab[at[o]] = block(BACK, at[o], 1)
        returned.append(wire(ab.at[at[o]], att.at[x], {"x": at[o]}))
    att[x] = block(BACK, x, 1)

    for copy in local[4:]:
        copy.wait()
    tag_row = tags[...]
    tag_col = to_column(tag_row)
    rank = jnp.sum(
        jnp.where(
            (tag_col == tag_row) & (iota((ROWS, ROWS), 0) < iota((ROWS, ROWS), 1)), 1.0, 0.0
        ),
        axis=0,
        keepdims=True,
    ).astype(jnp.int32)
    place = iota((CAP, ROWS), 0)
    landed(returned)
    flow = resid[...].astype(F32) + jnp.concatenate(
        [att[i].astype(F32) for i in range(NX)], axis=1
    )
    stream[...] = flow
    sqb[t] = to_row(jnp.sum(flow * flow, axis=1, keepdims=True))
    peers = [around(t, o, 8) for o in range(1, 8)]
    coming = [wire(sqb.at[t], sqb.at[t], {"y": lax.div(p, 2), "c": lax.rem(p, 2)}) for p in peers]
    gains = jnp.where(
        tag_col == 0, gain[0:1, :], jnp.where(tag_col == 1, gain[1:2, :], gain[2:3, :])
    )
    landed(coming)
    inv = to_column(lax.rsqrt(jnp.sum(sqb[...], axis=0) / D + 1e-5))
    normed = (flow * inv * gains).astype(BF16)
    for m in range(MODS):
        placing = jnp.where((tag_row == m) & (rank == place), 1.0, 0.0).astype(BF16)
        rows = jnp.dot(placing, normed, preferred_element_type=F32).astype(BF16)
        if m == WHOLE:
            xf[lax.div(z, 2), lax.rem(z, 2), x] = rows
        else:
            xb[m, lax.div(z, 2), lax.rem(z, 2), lax.div(x, 2)] = rows


def gather(wire, axis, n, me, view):
    half = n // 2
    for s in range(1, half + 1):
        last = s == half
        right = view(around(me, 1 - s, n), 0 if last else None)
        left = view(around(me, s - 1, n), 1 if last else None)
        moving = [
            wire(right, right, {axis: around(me, 1, n)}),
            wire(left, left, {axis: around(me, -1, n)}),
        ]
        yield
        landed(moving)


def scatter(wire, axis, n, me, view, landing):
    half = n // 2
    for s in range(1, half + 1):
        far = half - s + 1
        part = (0, 1) if s == 1 else (None, None)
        to = (around(me, far, n), around(me, -far, n))
        if s > 1:
            before = (0, 1) if s == 2 else (None, None)
            for side in (0, 1):
                total = view(to[side], before[side])
                total[...] = total[...] + landing(side * half + s - 2, before[side])[...]
        moving = [
            wire(
                view(to[side], part[side]),
                landing(side * half + s - 1, part[side]),
                {axis: around(me, by, n)},
            )
            for side, by in ((0, 1), (1, -1))
        ]
        yield
        landed(moving)
    total = view(me, None)
    total[...] = (
        total[...].astype(F32)
        + landing(half - 1, None)[...].astype(F32)
        + landing(n - 1, None)[...].astype(F32)
    ).astype(BF16)


def side_cut(base, part):
    return pl.ds(base, HALF) if part is None else pl.ds(base + 128 * part, 128)


def feed_forward(wire, here, weights, xb, xf, scratch):
    z, x, y, c = here
    pb, cr, ya, yb, hb, yo, za, xa, zt, xt, yf, zf, xs, zs, xf2, fin = scratch
    gate_w, up_w, down_w, ready = weights
    k = lax.div(x, 2)
    twin = {"x": around(x, 2, NX)}
    other = {"c": 1 - c}
    y_right, y_left = {"y": around(y, 1, NY)}, {"y": around(y, -1, NY)}
    rows_of = PAIR * CAP

    def plane(j):
        return lax.div(j, 2), lax.rem(j, 2)

    def rows_first(m):
        mine = xb.at[(m, *plane(z), k, slice(None), pl.ds(0, HALF))]
        moving = [wire(mine, mine, twin)]
        yield
        landed(moving)
        yield from gather(
            wire, "z", NZ, z,
            lambda j, p: xb.at[(m, *plane(j), slice(None), slice(None), side_cut(0, p))],
        )

    def rows_second(m):
        yield from gather(
            wire, "z", NZ, z,
            lambda j, p: xb.at[(m, *plane(j), k, slice(None), side_cut(HALF, p))],
        )
        mine = xb.at[m, :, :, k, :, pl.ds(HALF, HALF)]
        moving = [wire(mine, mine, twin)]
        yield
        landed(moving)

    def whole_first():
        row = plane(z)
        mine = xf.at[(*row, x, slice(None), pl.ds(0, HALF))]
        moving = [wire(mine, mine, {"x": around(x, o, NX)}) for o in (2, 1, 3)]
        yield
        landed(moving)
        yield from gather(
            wire, "z", NZ, z,
            lambda j, p: xf.at[(*plane(j), slice(None), slice(None), side_cut(0, p))],
        )

    def whole_second():
        yield from gather(
            wire, "z", NZ, z, lambda j, p: xf.at[(*plane(j), x, slice(None), side_cut(HALF, p))]
        )
        yield from gather(wire, "x", NX, x, lambda j, p: xf.at[:, :, j, :, side_cut(HALF, p)])

    def partial(m, e, core, side):
        if m == WHOLE:
            rows = xf[:, core, PAIR * e : PAIR * (e + 1)]
            w = (gate_w, up_w)[side][0, m]
        else:
            rows = xb[m, :, core]
            w = (gate_w, up_w)[side][e, m]
        rows = rows.reshape(NY * rows_of, 512)
        value = lax.dot_general(
            rows, w, (((1,), (1,)), ((), ())), preferred_element_type=F32
        )
        pb[m, e, :, core, :, side * WIDE : side * WIDE + UNITS] = value.astype(BF16).reshape(
            NY, rows_of, UNITS
        )

    def hidden(m, e):
        ready(m, e)
        at = {o: around(y, o, NY) for o in range(NY)}
        core = []
        for side in (0, 1):
            partial(m, e, 1 - c, side)
            cols = pl.ds(side * WIDE, WIDE)
            core.append(wire(pb.at[m, e, :, 1 - c, :, cols], cr.at[m, e, :, :, cols], other))
        yield
        partial(m, e, c, 0)
        partial(m, e, c, 1)
        landed(core)
        pb[m, e, at[2], c] = pb[m, e, at[2], c] + cr[m, e, at[2]]
        moving = [
            wire(pb.at[m, e, at[2], c, :, pl.ds(0, WIDE)], ya.at[m, e, 0], y_right),
            wire(pb.at[m, e, at[2], c, :, pl.ds(WIDE, WIDE)], ya.at[m, e, 1], y_left),
        ]
        for o in (1, 3):
            pb[m, e, at[o], c] = pb[m, e, at[o], c] + cr[m, e, at[o]]
        yield
        landed(moving)
        pb[m, e, at[1], c, :, 0:WIDE] = pb[m, e, at[1], c, :, 0:WIDE] + ya[m, e, 0]
        moving = [wire(pb.at[m, e, at[1], c], yb.at[m, e, 0], y_right)]
        pb[m, e, at[3], c, :, WIDE:] = pb[m, e, at[3], c, :, WIDE:] + ya[m, e, 1]
        moving.append(wire(pb.at[m, e, at[3], c], yb.at[m, e, 1], y_left))
        yield
        landed(moving)
        both = (
            pb[m, e, y, c].astype(F32)
            + cr[m, e, y].astype(F32)
            + yb[m, e, 0].astype(F32)
            + yb[m, e, 1].astype(F32)
        )
        gate, up = both[:, :WIDE], both[:, WIDE:]
        hb[m, e, y, c] = (gate / (1.0 + jnp.exp(-gate)) * up).astype(BF16)

        def pass_on(o, to, first=None):
            ref = hb.at[m, e, at[o], c]
            if first is not None:
                ref = hb.at[m, e, at[o], c, pl.ds(first, CAP)]
            return wire(ref, ref, to)

        moving = [pass_on(0, y_right), pass_on(0, y_left)]
        across = [pass_on(0, other)]
        yield
        landed(moving)
        moving = [pass_on(3, y_right, 0), pass_on(1, y_left, CAP)]
        across += [pass_on(3, other), pass_on(1, other)]
        yield
        landed(moving)
        across.append(pass_on(2, other))
        landed(across)

    summed = []

    def products_of(m):
        if m in summed:
            return
        summed.append(m)
        for core in (0, 1):
            part = jnp.zeros((NY * rows_of, 512), F32)
            for e in (0, 1):
                rows = hb[m, e, :, core].reshape(NY * rows_of, WIDE)[:, :UNITS]
                part = part + jnp.dot(rows, down_w[e, m], preferred_element_type=F32)
            yo[m, :, core] = part.astype(BF16).reshape(NY, PAIR, CAP, 512)

    def out_first(m):
        products_of(m)
        yield from scatter(
            wire, "z", NZ, z,
            lambda j, p: yo.at[(m, *plane(j), slice(None), slice(None), side_cut(0, p))],
            lambda n, p: za.at[m, n, :, :, side_cut(0, p)],
        )
        source = yo.at[(m, *plane(z), 1 - k, slice(None), pl.ds(0, HALF))]
        moving = [wire(source, xa.at[m], twin)]
        yield
        landed(moving)
        fin[m, :, 0:HALF] = yo[(m, *plane(z), k, slice(None), slice(0, HALF))] + xa[m]

    def out_second(m):
        products_of(m)
        moving = [wire(yo.at[m, :, :, 1 - k, :, pl.ds(HALF, HALF)], xt.at[m], twin)]
        yield
        landed(moving)
        right = slice(HALF, 2 * HALF)
        yo[m, :, :, k, :, right] = yo[m, :, :, k, :, right] + xt[m]
        yield from scatter(
            wire, "z", NZ, z,
            lambda j, p: yo.at[(m, *plane(j), k, slice(None), side_cut(HALF, p))],
            lambda n, p: zt.at[m, n, :, side_cut(0, p)],
        )
        fin[m, :, right] = yo[(m, *plane(z), k, slice(None), right)]

    made = []

    def products():
        if made:
            return
        made.append(True)
        for core in (0, 1):
            for e in (0, 1):
                rows = hb[WHOLE, e, :, core].reshape(NY * rows_of, WIDE)[:, :UNITS]
                part = jnp.dot(rows, down_w[0, WHOLE], preferred_element_type=F32)
                yf[:, core, PAIR * e : PAIR * (e + 1)] = part.astype(BF16).reshape(
                    NY, PAIR, CAP, 512
                )

    def whole_out_first():
        products()
        yield from scatter(
            wire, "z", NZ, z,
            lambda j, p: yf.at[(*plane(j), slice(None), slice(None), side_cut(0, p))],
            lambda n, p: zf.at[n, :, :, side_cut(0, p)],
        )
        moving = []
        for o in (2, 1, 3):
            to = around(x, o, NX)
            source = yf.at[(*plane(z), to, slice(None), pl.ds(0, HALF))]
            moving.append(wire(source, xs.at[o], {"x": to}))
        yield
        landed(moving)
        total = yf[(*plane(z), x, slice(None), slice(0, HALF))].astype(F32)
        for o in (1, 2, 3):
            total = total + xs[o].astype(F32)
        fin[WHOLE, :, 0:HALF] = total.astype(BF16)

    def whole_out_second():
        products()
        yield from scatter(
            wire, "x", NX, x,
            lambda j, p: yf.at[:, :, j, :, side_cut(HALF, p)],
            lambda n, p: xf2.at[n, :, :, :, side_cut(0, p)],
        )
        yield from scatter(
            wire, "z", NZ, z,
            lambda j, p: yf.at[(*plane(j), x, slice(None), side_cut(HALF, p))],
            lambda n, p: zs.at[n, :, side_cut(0, p)],
        )
        fin[WHOLE, :, HALF : 2 * HALF] = yf[(*plane(z), x, slice(None), slice(HALF, 2 * HALF))]

    work = [rows_first(0), whole_first(), rows_first(2)]
    work += [hidden(m, e) for m in range(MODS) for e in (0, 1)]
    work += [out_first(0), whole_out_first(), out_first(2), whole_second(), whole_out_second()]
    work += [rows_second(0), rows_second(2), out_second(0), out_second(2)]
    for n in ORDER:
        next(work[n], None)
    for process in work:
        for _ in process:
            pass


def layer_kernel(*args):
    refs, args = args[:7], args[7:]
    (gate_ref, up_ref, down_ref, out_ref), args = args[:4], args[4:]
    (send, recv, local), args = args[:3], args[3:]
    (xb, xf, stream, gate_w, up_w, down_w), args = args[:6], args[6:]
    attend_scratch, ffn_scratch = args[:16], args[16:]
    here = z, x, y, c = tuple(lax.axis_index(a) for a in ("z", "x", "y", "c"))
    peers = [around(2 * y + c, o, 8) for o in range(1, 8)]
    fetched = []

    def fetch(src, dst):
        copy = pltpu.make_async_copy(src, dst, local.at[len(fetched)])
        fetched.append(copy)
        copy.start()
        return copy

    greet(
        [{"x": around(x, o, NX)} for o in range(1, NX)]
        + [{"z": around(z, o, NZ)} for o in (1, -1)]
        + [{"y": lax.div(p, 2), "c": lax.rem(p, 2)} for p in peers]
    )
    wire = Wire(send, recv)
    tags, stream_ref, fin = attend_scratch[14], stream, ffn_scratch[-1]
    right, left = {"x": around(x, 1, NX)}, {"x": around(x, -1, NX)}
    weights = ((gate_ref, gate_w), (up_ref, up_w), (down_ref, down_w))
    own, lent = [], {}

    def lend():
        for m in (0, 2):
            to = left if m == 2 else right
            lent[m] = [wire(src.at[m], dst.at[1, m], to) for src, dst in weights]
        for src, dst in weights:
            own.append(fetch(src, dst.at[0]))

    def ready(m, e):
        if e == 1 and m != WHOLE:
            landed(lent[m])
        while own:
            own.pop().wait()

    attend(wire, here, refs, fetch, lend, xb, xf, stream_ref, attend_scratch)
    feed_forward(wire, here, (gate_w, up_w, down_w, ready), xb, xf, ffn_scratch)

    tag_row = tags[...]
    tag_col = to_column(tag_row)
    rank = jnp.sum(
        jnp.where(
            (tag_col == tag_row) & (iota((ROWS, ROWS), 1) < iota((ROWS, ROWS), 0)), 1.0, 0.0
        ),
        axis=1,
        keepdims=True,
    ).astype(jnp.int32)
    slot = iota((ROWS, CAP), 1)
    result = stream[...]
    for m in range(MODS):
        placing = jnp.where((tag_col == m) & (rank == slot), 1.0, 0.0).astype(BF16)
        result = result + jnp.dot(placing, fin[m], preferred_element_type=F32)
    out_ref[...] = result.astype(BF16)
    wire.drain()


def on_device(resid, queries, keys, values, doc_ids, modality, norm_gain, gate_w, up_w, down_w):
    block = (NX, ROWS, DH)
    i32 = jnp.int32
    shapes = [
        ((MODS, NY, 2, PAIR, CAP, 512), BF16),
        ((NY, 2, NX, CAP, 512), BF16),
        ((ROWS, 512), F32),
        ((2, MODS, UNITS, 512), BF16),
        ((2, MODS, UNITS, 512), BF16),
        ((2, MODS, UNITS, 512), BF16),
        (block, BF16),
        ((BACK + 1, *block), BF16),
        ((BACK + 1, *block), BF16),
        ((BACK - 1, TURNED, ROWS, DH), BF16),
        ((BACK - 1, TURNED, ROWS, DH), BF16),
        ((BACK + 1, NX, 1, ROWS), i32),
        ((NX, ROWS, 1), i32),
        ((NX, ROWS, 1), F32),
        ((NX, ROWS, 1), F32),
        (block, F32),
        (block, BF16),
        (block, BF16),
        ((8, 1, ROWS), F32),
        ((ROWS, 512), BF16),
        ((1, ROWS), i32),
        ((MODS, 512), F32),
        ((MODS, 2, NY, 2, PAIR * CAP, 2 * WIDE), BF16),
        ((MODS, 2, NY, PAIR * CAP, 2 * WIDE), BF16),
        ((MODS, 2, 2, PAIR * CAP, WIDE), BF16),
        ((MODS, 2, 2, PAIR * CAP, 2 * WIDE), BF16),
        ((MODS, 2, NY, 2, PAIR * CAP, WIDE), BF16),
        ((MODS, NY, 2, PAIR, CAP, 512), BF16),
        ((MODS, NZ, PAIR, CAP, HALF), BF16),
        ((MODS, CAP, HALF), BF16),
        ((MODS, NZ, CAP, HALF), BF16),
        ((MODS, NY, 2, CAP, HALF), BF16),
        ((NY, 2, NX, CAP, 512), BF16),
        ((NZ, NX, CAP, HALF), BF16),
        ((NX, CAP, HALF), BF16),
        ((NZ, CAP, HALF), BF16),
        ((NX, NY, 2, CAP, HALF), BF16),
        ((MODS, CAP, 512), BF16),
    ]
    dma = pltpu.SemaphoreType.DMA
    return pl.pallas_call(
        layer_kernel,
        out_shape=jax.ShapeDtypeStruct((ROWS, 512), BF16),
        in_specs=[pl.BlockSpec(memory_space=pl.ANY)] * 10,
        out_specs=pl.BlockSpec(memory_space=pltpu.VMEM),
        scratch_shapes=[dma((320,)), dma((320,)), dma((12,))]
        + [pltpu.VMEM(shape, kind) for shape, kind in shapes],
        compiler_params=pltpu.CompilerParams(
            collective_id=0, has_side_effects=True, vmem_limit_bytes=60 << 20
        ),
        name="layer",
    )(
        queries,
        keys,
        values,
        resid,
        doc_ids.reshape(1, ROWS),
        modality.reshape(1, ROWS),
        norm_gain,
        gate_w.transpose(1, 2, 0),
        up_w.transpose(1, 2, 0),
        down_w,
    )


def solution(mesh):
    split = Mesh(mesh.devices.reshape(NZ, NX, NY, 2), ("z", "x", "y", "c"))
    placed = (
        P(SEQ, TENSOR),
        P(SEQ, TENSOR),
        P(SEQ, TENSOR),
        P(SEQ, TENSOR),
        P(SEQ),
        P(SEQ),
        P(None, TENSOR),
        P(TENSOR, None, SEQ),
        P(TENSOR, None, SEQ),
        P(None, SEQ, TENSOR),
    )
    return jax.shard_map(
        on_device, mesh=split, in_specs=placed, out_specs=P(SEQ, TENSOR), check_vma=False
    )
```

```python
import math

import jax
import jax.numpy as jnp
from jax import lax
from jax.experimental import pallas as pl
from jax.experimental.pallas import tpu as pltpu
from jax.sharding import Mesh
from jax.sharding import PartitionSpec as P

D = 4096
DH = 128
MODS = 3
CAP = 48
ROWS = 128
NZ, NX, NY = 8, 4, 4
BACK = 4
TURNED = 3
UNITS, WIDE = 344, 384
HALF = 256
PAIR = 2
WHOLE = 1
ORDER = (
    15, 2, 12, 15, 12, 2, 15, 12, 2, 1, 15, 12, 2, 15, 12, 1, 2, 14, 1, 2, 0, 15, 7, 8,
    14, 7, 8, 1, 12, 0, 14, 7, 8, 1, 12, 0, 14, 7, 1, 5, 6, 0, 14, 8, 5, 7, 6, 0,
    8, 5, 0, 7, 14, 4, 6, 8, 17, 5, 11, 4, 3, 6, 11, 5, 3, 4, 17, 11, 6, 5, 3, 17,
    11, 4, 17, 6, 10, 11, 17, 3, 13, 4, 10, 11, 17, 3, 13, 4, 10, 3, 16, 9, 13, 10, 9, 13,
    10, 16, 9, 13, 16, 10, 9, 13, 16, 9, 13, 16, 9, 16,
)
SEQ = ("z", "x")
TENSOR = ("y", "c")
MESH = pl.DeviceIdType.MESH
F32, BF16 = jnp.float32, jnp.bfloat16


def around(i, by, n):
    return lax.rem(i + (by % n), n)


class Wire:
    def __init__(self, send, recv):
        self.send, self.recv, self.copies = send, recv, []

    def __call__(self, src, dst, to):
        k = len(self.copies)
        copy = pltpu.make_async_remote_copy(
            src_ref=src,
            dst_ref=dst,
            send_sem=self.send.at[k],
            recv_sem=self.recv.at[k],
            device_id=to,
            device_id_type=MESH,
        )
        self.copies.append(copy)
        copy.start()
        return copy

    def drain(self):
        for copy in self.copies:
            copy.wait_send()


def landed(copies):
    for copy in copies:
        copy.wait_recv()


def greet(partners):
    barrier = pltpu.get_barrier_semaphore()
    for partner in partners:
        pl.semaphore_signal(barrier, inc=1, device_id=partner, device_id_type=MESH)
    pl.semaphore_wait(barrier, len(partners))


def iota(shape, dim):
    return lax.broadcasted_iota(jnp.int32, shape, dim)


def eye():
    return iota((ROWS, ROWS), 0) == iota((ROWS, ROWS), 1)


def to_column(row):
    return jnp.sum(jnp.where(eye(), row, jnp.zeros_like(row)), axis=1, keepdims=True)


def to_row(column):
    return jnp.sum(jnp.where(eye(), column, jnp.zeros_like(column)), axis=0, keepdims=True)


def attend(wire, here, refs, fetch, lend, xb, xf, stream, scratch):
    z, x, y, c = here
    q_ref, k_ref, v_ref, resid_ref, docs_ref, tags_ref, gain_ref = refs
    qb, kb, vb, kr, vr, db, dcol, top, total, acc, ab, att, sqb, resid, tags, gain = scratch
    t = 2 * y + c
    up, down = {"z": around(z, 1, NZ)}, {"z": around(z, -1, NZ)}
    order = (2, 1, 3, 0)
    at = {o: around(x, o, NX) for o in order}

    def cols(p):
        return pl.ds(pl.multiple_of(p * DH, DH), DH)

    local = [
        fetch(k_ref.at[:, cols(x)], kb.at[0, x]),
        fetch(v_ref.at[:, cols(x)], vb.at[0, x]),
        fetch(docs_ref, db.at[0, x]),
        fetch(q_ref.at[:, cols(x)], qb.at[x]),
        fetch(tags_ref, tags),
        fetch(gain_ref, gain),
        fetch(resid_ref, resid),
    ]
    greet(
        [{"x": around(x, o, NX)} for o in range(1, NX)]
        + [{"z": around(z, o, NZ)} for o in (1, -1)]
        + [{"y": lax.div(p, 2), "c": lax.rem(p, 2)} for p in (around(t, o, 8) for o in range(1, 8))]
    )
    sides = ((k_ref, kb, kr), (v_ref, vb, vr))
    coming, asked = {}, []
    for o in order[:3]:
        coming[o] = [wire(ref.at[:, cols(at[o])], b.at[0, x], {"x": at[o]}) for ref, b, _ in sides]
    slot = {o: around(x, -o, NX) for o in order}
    rising = {0: [wire(ref.at[:, cols(x)], b.at[1, x], up) for ref, b, _ in sides]}
    falling = {}
    for o in order[:3]:
        asked.append(wire(docs_ref, db.at[0, x], {"x": at[o]}))
        asked.append(wire(q_ref.at[:, cols(at[o])], qb.at[x], {"x": at[o]}))
    lend()

    for o in order[:3]:
        rising[o], falling[o] = [], []
        for copy, (_, b, r) in zip(coming[o], sides):
            copy.wait_recv()
            rising[o].append(wire(b.at[0, slot[o]], b.at[1, slot[o]], up))
            falling[o].append(wire(b.at[0, slot[o]], r.at[0, o - 1], down))

    def pass_on(d, o):
        came, fell = rising.pop(o, []), falling.pop(o, [])
        landed(came + fell)
        if d == BACK:
            return
        rising[o], falling[o] = [], []
        for _, b, r in sides:
            if d + 1 < BACK or o == 0:
                rising[o].append(wire(b.at[d, slot[o]], b.at[d + 1, slot[o]], up))
            if o > 0:
                target = b.at[BACK, slot[o]] if d + 1 == BACK else r.at[d, o - 1]
                falling[o].append(wire(r.at[d - 1, o - 1], target, down))

    local[0].wait()
    local[1].wait()
    local[2].wait()
    local[3].wait()
    landed(asked)
    moving_d = [wire(db.at[0], db.at[1], up)]
    for o in order:
        dcol[at[o]] = to_column(db[0, at[o]])
    factor = math.log2(math.e) / math.sqrt(DH)
    returned = []

    def block(d, j, n):
        some, rows = pl.ds(j, n), n * ROWS
        keys = kb[d].reshape(NX * ROWS, DH)
        vals = vb[d].reshape(NX * ROWS, DH)
        key_docs = jnp.concatenate([db[d, i] for i in range(NX)], axis=1)
        score = lax.dot_general(
            qb[some].reshape(rows, DH), keys, (((1,), (1,)), ((), ())), preferred_element_type=F32
        )
        if d == 0:
            allowed = (iota(score.shape, 1) <= j * ROWS + iota(score.shape, 0)) & (
                key_docs == dcol[some].reshape(rows, 1)
            )
        else:
            allowed = jnp.where(z < d, -1, key_docs) == dcol[some].reshape(rows, 1)
        score = jnp.where(allowed, score, -1e30)
        high = jnp.max(score, axis=1, keepdims=True)
        if d > 0:
            old = top[some].reshape(rows, 1)
            high = jnp.maximum(high, old)
        power = jnp.exp2((score - high) * factor)
        add = jnp.sum(power, axis=1, keepdims=True)
        blend = jnp.dot(power.astype(BF16), vals, preferred_element_type=F32)
        if d > 0:
            fade = jnp.exp2((old - high) * factor)
            add = add + fade * total[some].reshape(rows, 1)
            blend = blend + fade * acc[some].reshape(rows, DH)
        if d < BACK:
            top[some] = high.reshape(n, ROWS, 1)
            total[some] = add.reshape(n, ROWS, 1)
            acc[some] = blend.reshape(n, ROWS, DH)
            return None
        return (blend / add).astype(BF16)

    for d in range(1, BACK + 1):
        pass_on(d, 0)
        pass_on(d, 2)
        block(d - 1, 0, 2)
        pass_on(d, 1)
        pass_on(d, 3)
        landed(moving_d)
        if d < BACK:
            moving_d = [wire(db.at[d], db.at[d + 1], up)]
        block(d - 1, 2, 2)
    for o in order[:3]:
        ab[at[o]] = block(BACK, at[o], 1)
        returned.append(wire(ab.at[at[o]], att.at[x], {"x": at[o]}))
    att[x] = block(BACK, x, 1)

    for copy in local[4:]:
        copy.wait()
    tag_row = tags[...]
    tag_col = to_column(tag_row)
    rank = jnp.sum(
        jnp.where(
            (tag_col == tag_row) & (iota((ROWS, ROWS), 0) < iota((ROWS, ROWS), 1)), 1.0, 0.0
        ),
        axis=0,
        keepdims=True,
    ).astype(jnp.int32)
    place = iota((CAP, ROWS), 0)
    landed(returned)
    flow = resid[...].astype(F32) + jnp.concatenate(
        [att[i].astype(F32) for i in range(NX)], axis=1
    )
    stream[...] = flow
    sqb[t] = to_row(jnp.sum(flow * flow, axis=1, keepdims=True))
    peers = [around(t, o, 8) for o in (4, 3, 5, 2, 6, 1, 7)]
    coming = [wire(sqb.at[t], sqb.at[t], {"y": lax.div(p, 2), "c": lax.rem(p, 2)}) for p in peers]
    gains = jnp.where(
        tag_col == 0, gain[0:1, :], jnp.where(tag_col == 1, gain[1:2, :], gain[2:3, :])
    )
    landed(coming)
    inv = to_column(lax.rsqrt(jnp.sum(sqb[...], axis=0) / D + 1e-5))
    normed = (flow * inv * gains).astype(BF16)
    for m in range(MODS):
        placing = jnp.where((tag_row == m) & (rank == place), 1.0, 0.0).astype(BF16)
        rows = jnp.dot(placing, normed, preferred_element_type=F32).astype(BF16)
        if m == WHOLE:
            xf[lax.div(z, 2), lax.rem(z, 2), x] = rows
        else:
            xb[m, lax.div(z, 2), lax.rem(z, 2), lax.div(x, 2)] = rows


def gather(wire, axis, n, me, view):
    half = n // 2
    for s in range(1, half + 1):
        last = s == half
        right = view(around(me, 1 - s, n), 0 if last else None)
        left = view(around(me, s - 1, n), 1 if last else None)
        moving = [
            wire(right, right, {axis: around(me, 1, n)}),
            wire(left, left, {axis: around(me, -1, n)}),
        ]
        yield
        landed(moving)


def scatter(wire, axis, n, me, view, landing):
    half = n // 2
    for s in range(1, half + 1):
        far = half - s + 1
        part = (0, 1) if s == 1 else (None, None)
        to = (around(me, far, n), around(me, -far, n))
        if s > 1:
            before = (0, 1) if s == 2 else (None, None)
            for side in (0, 1):
                total = view(to[side], before[side])
                total[...] = total[...] + landing(side * half + s - 2, before[side])[...]
        moving = [
            wire(
                view(to[side], part[side]),
                landing(side * half + s - 1, part[side]),
                {axis: around(me, by, n)},
            )
            for side, by in ((0, 1), (1, -1))
        ]
        yield
        landed(moving)
    total = view(me, None)
    total[...] = (
        total[...].astype(F32)
        + landing(half - 1, None)[...].astype(F32)
        + landing(n - 1, None)[...].astype(F32)
    ).astype(BF16)


def side_cut(base, part):
    return pl.ds(base, HALF) if part is None else pl.ds(base + 128 * part, 128)


def feed_forward(wire, here, weights, xb, xf, scratch):
    z, x, y, c = here
    pb, cr, ya, yb, hb, yo, za, xa, zt, xt, yf, zf, xs, zs, xf2, fin = scratch
    gate_w, up_w, down_w, ready = weights
    k = lax.div(x, 2)
    twin = {"x": around(x, 2, NX)}
    other = {"c": 1 - c}
    y_right, y_left = {"y": around(y, 1, NY)}, {"y": around(y, -1, NY)}
    rows_of = PAIR * CAP

    def plane(j):
        return lax.div(j, 2), lax.rem(j, 2)

    def rows_first(m):
        mine = xb.at[(m, *plane(z), k, slice(None), pl.ds(0, HALF))]
        moving = [wire(mine, mine, twin)]
        yield
        landed(moving)
        yield from gather(
            wire, "z", NZ, z,
            lambda j, p: xb.at[(m, *plane(j), slice(None), slice(None), side_cut(0, p))],
        )

    def rows_second(m):
        yield from gather(
            wire, "z", NZ, z,
            lambda j, p: xb.at[(m, *plane(j), k, slice(None), side_cut(HALF, p))],
        )
        mine = xb.at[m, :, :, k, :, pl.ds(HALF, HALF)]
        moving = [wire(mine, mine, twin)]
        yield
        landed(moving)

    def whole_first():
        row = plane(z)
        mine = xf.at[(*row, x, slice(None), pl.ds(0, HALF))]
        moving = [wire(mine, mine, {"x": around(x, o, NX)}) for o in (2, 1, 3)]
        yield
        landed(moving)
        yield from gather(
            wire, "z", NZ, z,
            lambda j, p: xf.at[(*plane(j), slice(None), slice(None), side_cut(0, p))],
        )

    def whole_second():
        yield from gather(
            wire, "z", NZ, z, lambda j, p: xf.at[(*plane(j), x, slice(None), side_cut(HALF, p))]
        )
        yield from gather(wire, "x", NX, x, lambda j, p: xf.at[:, :, j, :, side_cut(HALF, p)])

    def partial(m, e, core, side):
        if m == WHOLE:
            rows = xf[:, core, PAIR * e : PAIR * (e + 1)]
            w = (gate_w, up_w)[side][0, m]
        else:
            rows = xb[m, :, core]
            w = (gate_w, up_w)[side][e, m]
        rows = rows.reshape(NY * rows_of, 512)
        value = lax.dot_general(
            rows, w, (((1,), (1,)), ((), ())), preferred_element_type=F32
        )
        pb[m, e, :, core, :, side * WIDE : side * WIDE + UNITS] = value.astype(BF16).reshape(
            NY, rows_of, UNITS
        )

    def hidden(m, e):
        ready(m, e)
        at = {o: around(y, o, NY) for o in range(NY)}
        core = []
        for side in (0, 1):
            partial(m, e, 1 - c, side)
            cols = pl.ds(side * WIDE, WIDE)
            core.append(wire(pb.at[m, e, :, 1 - c, :, cols], cr.at[m, e, :, :, cols], other))
        yield
        partial(m, e, c, 0)
        partial(m, e, c, 1)
        landed(core)
        pb[m, e, at[2], c] = pb[m, e, at[2], c] + cr[m, e, at[2]]
        moving = [
            wire(pb.at[m, e, at[2], c, :, pl.ds(0, WIDE)], ya.at[m, e, 0], y_right),
            wire(pb.at[m, e, at[2], c, :, pl.ds(WIDE, WIDE)], ya.at[m, e, 1], y_left),
        ]
        for o in (1, 3):
            pb[m, e, at[o], c] = pb[m, e, at[o], c] + cr[m, e, at[o]]
        yield
        landed(moving)
        pb[m, e, at[1], c, :, 0:WIDE] = pb[m, e, at[1], c, :, 0:WIDE] + ya[m, e, 0]
        moving = [wire(pb.at[m, e, at[1], c], yb.at[m, e, 0], y_right)]
        pb[m, e, at[3], c, :, WIDE:] = pb[m, e, at[3], c, :, WIDE:] + ya[m, e, 1]
        moving.append(wire(pb.at[m, e, at[3], c], yb.at[m, e, 1], y_left))
        yield
        landed(moving)
        both = (
            pb[m, e, y, c].astype(F32)
            + cr[m, e, y].astype(F32)
            + yb[m, e, 0].astype(F32)
            + yb[m, e, 1].astype(F32)
        )
        gate, up = both[:, :WIDE], both[:, WIDE:]
        hb[m, e, y, c] = (gate / (1.0 + jnp.exp(-gate)) * up).astype(BF16)

        def pass_on(o, to, first=None):
            ref = hb.at[m, e, at[o], c]
            if first is not None:
                ref = hb.at[m, e, at[o], c, pl.ds(first, CAP)]
            return wire(ref, ref, to)

        moving = [pass_on(0, y_right), pass_on(0, y_left)]
        across = [pass_on(0, other)]
        yield
        landed(moving)
        moving = [pass_on(3, y_right, 0), pass_on(1, y_left, CAP)]
        across += [pass_on(3, other), pass_on(1, other)]
        yield
        landed(moving)
        across.append(pass_on(2, other))
        landed(across)

    summed = []

    def products_of(m):
        if m in summed:
            return
        summed.append(m)
        for core in (0, 1):
            part = jnp.zeros((NY * rows_of, 512), F32)
            for e in (0, 1):
                rows = hb[m, e, :, core].reshape(NY * rows_of, WIDE)[:, :UNITS]
                part = part + jnp.dot(rows, down_w[e, m], preferred_element_type=F32)
            yo[m, :, core] = part.astype(BF16).reshape(NY, PAIR, CAP, 512)

    def out_first(m):
        products_of(m)
        yield from scatter(
            wire, "z", NZ, z,
            lambda j, p: yo.at[(m, *plane(j), slice(None), slice(None), side_cut(0, p))],
            lambda n, p: za.at[m, n, :, :, side_cut(0, p)],
        )
        source = yo.at[(m, *plane(z), 1 - k, slice(None), pl.ds(0, HALF))]
        moving = [wire(source, xa.at[m], twin)]
        yield
        landed(moving)
        fin[m, :, 0:HALF] = yo[(m, *plane(z), k, slice(None), slice(0, HALF))] + xa[m]

    def out_second(m):
        products_of(m)
        moving = [wire(yo.at[m, :, :, 1 - k, :, pl.ds(HALF, HALF)], xt.at[m], twin)]
        yield
        landed(moving)
        right = slice(HALF, 2 * HALF)
        yo[m, :, :, k, :, right] = yo[m, :, :, k, :, right] + xt[m]
        yield from scatter(
            wire, "z", NZ, z,
            lambda j, p: yo.at[(m, *plane(j), k, slice(None), side_cut(HALF, p))],
            lambda n, p: zt.at[m, n, :, side_cut(0, p)],
        )
        fin[m, :, right] = yo[(m, *plane(z), k, slice(None), right)]

    made = []

    def products():
        if made:
            return
        made.append(True)
        for core in (0, 1):
            for e in (0, 1):
                rows = hb[WHOLE, e, :, core].reshape(NY * rows_of, WIDE)[:, :UNITS]
                part = jnp.dot(rows, down_w[0, WHOLE], preferred_element_type=F32)
                yf[:, core, PAIR * e : PAIR * (e + 1)] = part.astype(BF16).reshape(
                    NY, PAIR, CAP, 512
                )

    def whole_out_first():
        products()
        yield from scatter(
            wire, "z", NZ, z,
            lambda j, p: yf.at[(*plane(j), slice(None), slice(None), side_cut(0, p))],
            lambda n, p: zf.at[n, :, :, side_cut(0, p)],
        )
        moving = []
        for o in (2, 1, 3):
            to = around(x, o, NX)
            source = yf.at[(*plane(z), to, slice(None), pl.ds(0, HALF))]
            moving.append(wire(source, xs.at[o], {"x": to}))
        yield
        landed(moving)
        total = yf[(*plane(z), x, slice(None), slice(0, HALF))].astype(F32)
        for o in (1, 2, 3):
            total = total + xs[o].astype(F32)
        fin[WHOLE, :, 0:HALF] = total.astype(BF16)

    def whole_out_second():
        products()
        yield from scatter(
            wire, "x", NX, x,
            lambda j, p: yf.at[:, :, j, :, side_cut(HALF, p)],
            lambda n, p: xf2.at[n, :, :, :, side_cut(0, p)],
        )
        yield from scatter(
            wire, "z", NZ, z,
            lambda j, p: yf.at[(*plane(j), x, slice(None), side_cut(HALF, p))],
            lambda n, p: zs.at[n, :, side_cut(0, p)],
        )
        fin[WHOLE, :, HALF : 2 * HALF] = yf[(*plane(z), x, slice(None), slice(HALF, 2 * HALF))]

    work = [rows_first(0), whole_first(), rows_first(2)]
    work += [hidden(m, e) for m in range(MODS) for e in (0, 1)]
    work += [out_first(0), whole_out_first(), out_first(2), whole_second(), whole_out_second()]
    work += [rows_second(0), rows_second(2), out_second(0), out_second(2)]
    for n in ORDER:
        next(work[n], None)
    for process in work:
        for _ in process:
            pass


def layer_kernel(*args):
    refs, args = args[:7], args[7:]
    (gate_ref, up_ref, down_ref, out_ref), args = args[:4], args[4:]
    (send, recv, local), args = args[:3], args[3:]
    (xb, xf, stream, gate_w, up_w, down_w), args = args[:6], args[6:]
    attend_scratch, ffn_scratch = args[:16], args[16:]
    here = z, x, y, c = tuple(lax.axis_index(a) for a in ("z", "x", "y", "c"))
    fetched = []

    def fetch(src, dst):
        copy = pltpu.make_async_copy(src, dst, local.at[len(fetched)])
        fetched.append(copy)
        copy.start()
        return copy

    wire = Wire(send, recv)
    tags, stream_ref, fin = attend_scratch[14], stream, ffn_scratch[-1]
    right, left = {"x": around(x, 1, NX)}, {"x": around(x, -1, NX)}
    weights = ((gate_ref, gate_w), (up_ref, up_w), (down_ref, down_w))
    own, lent = [], {}

    def lend():
        for m in (0, 2):
            to = left if m == 2 else right
            lent[m] = [wire(src.at[m], dst.at[1, m], to) for src, dst in weights]
        for src, dst in weights:
            own.append(fetch(src, dst.at[0]))

    def ready(m, e):
        if e == 1 and m != WHOLE:
            landed(lent[m])
        while own:
            own.pop().wait()

    attend(wire, here, refs, fetch, lend, xb, xf, stream_ref, attend_scratch)
    feed_forward(wire, here, (gate_w, up_w, down_w, ready), xb, xf, ffn_scratch)

    tag_row = tags[...]
    tag_col = to_column(tag_row)
    rank = jnp.sum(
        jnp.where(
            (tag_col == tag_row) & (iota((ROWS, ROWS), 1) < iota((ROWS, ROWS), 0)), 1.0, 0.0
        ),
        axis=1,
        keepdims=True,
    ).astype(jnp.int32)
    slot = iota((ROWS, CAP), 1)
    result = stream[...]
    for m in range(MODS):
        placing = jnp.where((tag_col == m) & (rank == slot), 1.0, 0.0).astype(BF16)
        result = result + jnp.dot(placing, fin[m], preferred_element_type=F32)
    out_ref[...] = result.astype(BF16)
    wire.drain()


def on_device(resid, queries, keys, values, doc_ids, modality, norm_gain, gate_w, up_w, down_w):
    block = (NX, ROWS, DH)
    i32 = jnp.int32
    shapes = [
        ((MODS, NY, 2, PAIR, CAP, 512), BF16),
        ((NY, 2, NX, CAP, 512), BF16),
        ((ROWS, 512), F32),
        ((2, MODS, UNITS, 512), BF16),
        ((2, MODS, UNITS, 512), BF16),
        ((2, MODS, UNITS, 512), BF16),
        (block, BF16),
        ((BACK + 1, *block), BF16),
        ((BACK + 1, *block), BF16),
        ((BACK - 1, TURNED, ROWS, DH), BF16),
        ((BACK - 1, TURNED, ROWS, DH), BF16),
        ((BACK + 1, NX, 1, ROWS), i32),
        ((NX, ROWS, 1), i32),
        ((NX, ROWS, 1), F32),
        ((NX, ROWS, 1), F32),
        (block, F32),
        (block, BF16),
        (block, BF16),
        ((8, 1, ROWS), F32),
        ((ROWS, 512), BF16),
        ((1, ROWS), i32),
        ((MODS, 512), F32),
        ((MODS, 2, NY, 2, PAIR * CAP, 2 * WIDE), BF16),
        ((MODS, 2, NY, PAIR * CAP, 2 * WIDE), BF16),
        ((MODS, 2, 2, PAIR * CAP, WIDE), BF16),
        ((MODS, 2, 2, PAIR * CAP, 2 * WIDE), BF16),
        ((MODS, 2, NY, 2, PAIR * CAP, WIDE), BF16),
        ((MODS, NY, 2, PAIR, CAP, 512), BF16),
        ((MODS, NZ, PAIR, CAP, HALF), BF16),
        ((MODS, CAP, HALF), BF16),
        ((MODS, NZ, CAP, HALF), BF16),
        ((MODS, NY, 2, CAP, HALF), BF16),
        ((NY, 2, NX, CAP, 512), BF16),
        ((NZ, NX, CAP, HALF), BF16),
        ((NX, CAP, HALF), BF16),
        ((NZ, CAP, HALF), BF16),
        ((NX, NY, 2, CAP, HALF), BF16),
        ((MODS, CAP, 512), BF16),
    ]
    dma = pltpu.SemaphoreType.DMA
    return pl.pallas_call(
        layer_kernel,
        out_shape=jax.ShapeDtypeStruct((ROWS, 512), BF16),
        in_specs=[pl.BlockSpec(memory_space=pl.ANY)] * 10,
        out_specs=pl.BlockSpec(memory_space=pltpu.VMEM),
        scratch_shapes=[dma((320,)), dma((320,)), dma((12,))]
        + [pltpu.VMEM(shape, kind) for shape, kind in shapes],
        compiler_params=pltpu.CompilerParams(
            collective_id=0, has_side_effects=True, vmem_limit_bytes=60 << 20
        ),
        name="layer",
    )(
        queries,
        keys,
        values,
        resid,
        doc_ids.reshape(1, ROWS),
        modality.reshape(1, ROWS),
        norm_gain,
        gate_w.transpose(1, 2, 0),
        up_w.transpose(1, 2, 0),
        down_w,
    )


def solution(mesh):
    split = Mesh(mesh.devices.reshape(NZ, NX, NY, 2), ("z", "x", "y", "c"))
    placed = (
        P(SEQ, TENSOR),
        P(SEQ, TENSOR),
        P(SEQ, TENSOR),
        P(SEQ, TENSOR),
        P(SEQ),
        P(SEQ),
        P(None, TENSOR),
        P(TENSOR, None, SEQ),
        P(TENSOR, None, SEQ),
        P(None, SEQ, TENSOR),
    )
    return jax.shard_map(
        on_device, mesh=split, in_specs=placed, out_specs=P(SEQ, TENSOR), check_vma=False
    )
```
